32 devices in a mesh: pairs: 2 (over x), cols: 16 (over z, y, core).
Axes of the slice: x: 2, y: 2, z: 4, core: 2. Of those that a mesh axis runs over, the one named last changes fastest.
Arguments:
- new_points: bfloat16 [4096, 512], P('pairs'), parts along dimension 0, may hold values from -8 to 8
- arch_points: bfloat16 [32768, 512], P(('pairs', 'cols')), parts along dimension 0, may hold values from -4 to 4
- new_mass: float32 [4096], P('pairs'), parts along dimension 0, may hold values from 0.3 to 3
- arch_mass: float32 [32768], P(('pairs', 'cols')), parts along dimension 0, may hold values from 0.3 to 3
Outputs:
- new_potential: float32 [4096], P('pairs'), parts along dimension 0
- arch_potential: float32 [32768], P(('pairs', 'cols')), parts along dimension 0
- new_grad: float32 [4096, 512], P(('pairs', 'cols')), parts along dimension 0
- arch_grad: float32 [32768, 512], P(('pairs', 'cols')), parts along dimension 0
The draws below stay inside these ranges and needn't reach their ends.
There are 2 independent parts, one for each index of `pairs`. The reference program is written for one: setup_inputs(seed, part) draws one part's arguments, and reference() takes and returns one part's arrays. A program takes and returns all parts, laid end to end along the dimension named above; each array names one. Nothing has to cross between parts.
All inputs are finite; a program needn't handle non-finite values.
Results may differ from the reference program's by a relative error of at most 0.0028.
Values sent between devices are 32-bit elements; how exact they have to be, the bound alone decides.
No kernel may reach another device: no remote copies, remote signals or barrier semaphores. Data moves between devices by JAX's collectives and lax.ppermute only.
A program may use at most 64 MiB of HBM per device.

```python
import math
import jax
import jax.numpy as jnp
from jax import lax

D = 512
NEW_ROWS = 2048
ITERS = 3
ARCH = 16384


def draw_new_points(key, part):
    key = jax.random.fold_in(key, 11)
    first = jax.random.fold_in(key, 0)
    values = jnp.clip(jax.random.normal(first, (NEW_ROWS, D), jnp.float32), -4.0, 4.0)
    return values.astype(jnp.bfloat16)


def block_scale(rng, dims, cuts, low, top_value):
    def one(position, parts):
        heights = jax.random.uniform(jax.random.fold_in(jax.random.fold_in(rng, 6), position), (parts,), jnp.float32, low / len(cuts), top_value / len(cuts))
        return jnp.repeat(jnp.exp(heights), dims[position] // parts).reshape((-1,) + (1,) * (len(dims) - position - 1))

    level = one(*cuts[0])
    for cut in cuts[1:]:
        level = level * one(*cut)
    return level


def centred(key, dims, spread, most, cuts=(), dtype=jnp.bfloat16):
    level = block_scale(key, dims, cuts, -0.22, 0.18) if cuts else 1.0
    result = jax.random.normal(key, dims, jnp.float32) * spread * level
    return jnp.minimum(jnp.maximum(result, -most), most).astype(dtype)


def setup_inputs(seed: int = 0, part: int = 0) -> dict:
    splits = jax.random.split(jax.random.key(seed), 5)
    own_keys = jax.random.split(jax.random.fold_in(splits[4], part), 5)
    new_points = draw_new_points(jax.random.fold_in(jax.random.fold_in(splits[4], part), 71), part)
    arch_points = centred(own_keys[1], (ARCH, D), 1.0, 4.0, ((0, 16),))
    new_mass = jnp.clip(jnp.exp(jax.random.uniform(own_keys[2], (NEW_ROWS,), jnp.float32, math.log(0.3), math.log(3.0))), 0.3, 3.0)
    arch_mass = jnp.clip(jnp.exp(math.log(3.0) - 2.3025851 * jax.random.uniform(own_keys[3], (ARCH,), jnp.float32) ** block_scale(own_keys[3], (ARCH,), ((0, 16),), -0.2, 0.2)), 0.3, 3.0)
    return {"new_points": new_points, "arch_points": arch_points, "new_mass": new_mass, "arch_mass": arch_mass}


EPSILON = 0.05


def reference(new_points, arch_points, new_mass, arch_mass):
    new_float = new_points.astype(jnp.float32)
    arch_float = arch_points.astype(jnp.float32)
    sq_new = jnp.sum(new_float * new_float, 1)
    sq_arch = jnp.sum(arch_float * arch_float, 1)
    cross = lax.dot_general(new_points, arch_points, (((1,), (1,)), ((), ())), preferred_element_type=jnp.float32)
    cost = (sq_new[:, None] + sq_arch[None, :] - 2.0 * cross) / D
    log_new = jnp.log(new_mass / NEW_ROWS)
    log_arch = jnp.log(arch_mass / ARCH)
    arch_pot = jnp.zeros((ARCH,), jnp.float32)
    arch_hist = [arch_pot]
    new_hist = []
    for step in range(ITERS):
        scores = log_arch[None, :] + (arch_pot[None, :] - cost) / EPSILON
        top = jnp.max(scores, 1)
        total = jnp.sum(jnp.exp(scores - top[:, None]), 1)
        new_pot = -EPSILON * (top + jnp.log(total))
        weights = log_new[:, None] + (new_pot[:, None] - cost) / EPSILON
        col_top = jnp.max(weights, 0)
        arch_pot = -EPSILON * (col_top + jnp.log(jnp.sum(jnp.exp(weights - col_top[None, :]), 0)))
        new_hist.append(new_pot)
        arch_hist.append(arch_pot)
    arch_bar = arch_mass / ARCH
    cost_bar = jnp.zeros(cost.shape, jnp.float32)
    for step in reversed(range(ITERS)):
        new_pot = new_hist[step]
        q_tile = jnp.exp(log_new[:, None] + (new_pot[:, None] - cost + arch_hist[step + 1][None, :]) / EPSILON)
        w_tile = q_tile * arch_bar[None, :]
        cost_bar = cost_bar + w_tile
        new_bar = jnp.sum(w_tile, 1)
        if step == ITERS - 1:
            new_bar = new_bar + new_mass / NEW_ROWS
        p_tile = jnp.exp(log_arch[None, :] + (arch_hist[step][None, :] - cost + new_pot[:, None]) / EPSILON)
        v_tile = p_tile * new_bar[:, None]
        cost_bar = cost_bar + v_tile
        arch_bar = jnp.sum(v_tile, 0)
    bar_half = cost_bar.astype(jnp.bfloat16)
    row_weight = jnp.sum(cost_bar, 1)
    col_weight = jnp.sum(cost_bar, 0)
    new_grad = NEW_ROWS * (row_weight[:, None] * new_float - jnp.dot(bar_half, arch_points, preferred_element_type=jnp.float32))
    back = lax.dot_general(bar_half, new_points, (((0,), (0,)), ((), ())), preferred_element_type=jnp.float32)
    arch_grad = ARCH * (col_weight[:, None] * arch_float - back)
    return new_hist[-1], arch_hist[-1], new_grad, arch_grad
```

```python
import functools
import math
import jax
import jax.numpy as jnp
from jax import lax
from jax.experimental import pallas as pl
from jax.experimental.pallas import tpu as pltpu
from jax.sharding import PartitionSpec as P

EPSILON = 0.05
LOGK = math.log2(math.e) / EPSILON
LANES = 128
SUB = 8
VMEM = pltpu.VMEM
F32 = jnp.float32
BF16 = jnp.bfloat16


def params(mib=28):
    return pltpu.CompilerParams(vmem_limit_bytes=mib * 1024 * 1024)


def full(n):
    return [pl.BlockSpec(memory_space=VMEM)] * n


def column(row):
    return jnp.transpose(jnp.broadcast_to(row, (LANES, LANES)))


def lanes(x):
    return [x[:, l * LANES:(l + 1) * LANES] for l in range(x.shape[1] // LANES)]


def wide(x):
    return jnp.broadcast_to(x, (SUB, LANES))


def tree(op, xs):
    xs = list(xs)
    while len(xs) > 1:
        xs = [op(xs[i], xs[i + 1]) if i + 1 < len(xs) else xs[i] for i in range(0, len(xs), 2)]
    return xs[0]


def lane_sum(xs):
    return wide(jnp.sum(tree(jnp.add, xs), axis=1, keepdims=True))


def lane_max(xs):
    return wide(jnp.max(tree(jnp.maximum, xs), axis=1, keepdims=True))


def scores_kernel(total_cols, x_ref, y_ref, mass_ref, z_ref, b_ref, sq_ref, lse_ref, cb_ref):
    cols, width = y_ref.shape
    rows = x_ref.shape[0]
    for c in range(cols // LANES):
        s = pl.ds(c * LANES, LANES)
        b = column(mass_ref[:, s] * (1.0 / total_cols))
        b_ref[s, :] = b
        yf = y_ref[s, :].astype(F32)
        sq = jnp.sum(yf * yf, axis=1, keepdims=True) * (LOGK / width)
        sq = jnp.broadcast_to(sq, (LANES, LANES))
        sq_ref[s, :] = sq
        cb_ref[s, :] = jnp.log2(b) - sq
    step = 2 * LANES
    for r in range(rows // step):
        s = pl.ds(r * step, step)
        z_ref[:, s] = lax.dot_general(
            y_ref[...], x_ref[s, :], (((1,), (1,)), ((), ())), preferred_element_type=F32
        ) * (2.0 * LOGK / width)

        def top(g, m):
            q = pl.ds(pl.multiple_of(g * 64, 64), 64)
            cb = cb_ref[q, :]
            z = z_ref[q, s]
            for h in range(64 // SUB):
                hs = slice(h * SUB, (h + 1) * SUB)
                m = [jnp.maximum(a, v + cb[hs]) for a, v in zip(m, lanes(z[hs]))]
            return m

        first = [jnp.full((SUB, LANES), -jnp.inf, F32)] * (step // LANES)
        m = lax.fori_loop(0, cols // 64, top, first)
        m = [jnp.max(a, axis=0, keepdims=True) for a in m]
        mw = [wide(a) for a in m]

        def add(g, t):
            q = pl.ds(pl.multiple_of(g * 64, 64), 64)
            cb = cb_ref[q, :]
            z = z_ref[q, s]
            for h in range(64 // SUB):
                hs = slice(h * SUB, (h + 1) * SUB)
                t = [a + jnp.exp2(v + cb[hs] - n) for a, v, n in zip(t, lanes(z[hs]), mw)]
            return t

        t = lax.fori_loop(0, cols // 64, add, [jnp.zeros((SUB, LANES), F32)] * (step // LANES))
        for l, (n, v) in enumerate(zip(m, t)):
            lse_ref[:, pl.ds(r * step + l * LANES, LANES)] = n + jnp.log2(
                jnp.sum(v, axis=0, keepdims=True)
            )


def scores(new_points, arch_points, arch_mass, total_cols):
    rows, cols = new_points.shape[0], arch_points.shape[0]
    return pl.pallas_call(
        functools.partial(scores_kernel, total_cols),
        out_shape=(
            VMEM((cols, rows), F32),
            VMEM((cols, LANES), F32),
            VMEM((cols, LANES), F32),
            jax.ShapeDtypeStruct((1, rows), F32),
        ),
        in_specs=full(3),
        out_specs=tuple(full(4)),
        scratch_shapes=[pltpu.VMEM((cols, LANES), F32)],
        compiler_params=params(),
        name="scores",
    )(new_points, arch_points, arch_mass.reshape(1, cols))


def plan_kernel(z_ref, b_ref, sq_ref, w_ref, q_ref, beta_ref, vb_ref, part_ref):
    cols, rows = z_ref.shape
    w = [wide(a) for a in lanes(w_ref[...])]

    def body(g, acc):
        for h in range(2):
            s = pl.ds(pl.multiple_of(g * 2 * SUB, 2 * SUB) + h * SUB, SUB)
            e = [z + a for z, a in zip(lanes(z_ref[s, :]), w)]
            n = lane_max(e)
            e = [jnp.exp2(a - n) for a in e]
            t = lane_sum(e)
            beta = -(n + jnp.log2(t))
            r = 1.0 / t
            b = b_ref[s, :]
            beta_ref[s, :] = beta
            vb_ref[s, :] = b * jnp.exp2(-sq_ref[s, :] - beta)
            rb = []
            for l, a in enumerate(e):
                q = a * r
                q_ref[s, pl.ds(l * LANES, LANES)] = q
                rb.append(q)
            acc = [a + q * b for a, q in zip(acc, rb)]
        return acc

    acc = lax.fori_loop(0, cols // (2 * SUB), body, [jnp.zeros((SUB, LANES), F32)] * len(w))
    for l, a in enumerate(acc):
        part_ref[:, pl.ds(l * LANES, LANES)] = jnp.sum(a, axis=0, keepdims=True)


def plan(z, b, sq, w):
    cols, rows = z.shape
    return pl.pallas_call(
        plan_kernel,
        out_shape=(
            VMEM((cols, rows), F32),
            VMEM((cols, LANES), F32),
            VMEM((cols, LANES), F32),
            jax.ShapeDtypeStruct((1, rows), F32),
        ),
        in_specs=full(4),
        out_specs=tuple(full(4)),
        compiler_params=params(),
        name="plan",
    )(z, b, sq, w)


def sweep_kernel(kind, q_ref, b_ref, *refs):
    cols, rows = q_ref.shape
    v_ref = refs[0] if kind == "mid" else None
    w_ref, c_ref, part_ref = refs[-3:]
    w = [wide(a) for a in lanes(w_ref[...])]
    unroll = 4

    def body(g, acc):
        for h in range(unroll):
            s = pl.ds(pl.multiple_of(g * unroll * SUB, unroll * SUB) + h * SUB, SUB)
            q = lanes(q_ref[s, :])
            t = lane_sum([a * c for a, c in zip(q, w)])
            b = b_ref[s, :]
            if kind == "fwd":
                c = b / t
            elif kind == "mid":
                c = b * t * v_ref[s, :] * v_ref[s, :]
            else:
                c = b * t
            c_ref[s, :] = c
            acc = [a + d * c for a, d in zip(acc, q)]
        return acc

    acc = lax.fori_loop(0, cols // (unroll * SUB), body, [jnp.zeros((SUB, LANES), F32)] * len(w))
    for l, a in enumerate(acc):
        part_ref[:, pl.ds(l * LANES, LANES)] = jnp.sum(a, axis=0, keepdims=True)


def sweep(kind, q, b, w, *more):
    cols, rows = q.shape
    return pl.pallas_call(
        functools.partial(sweep_kernel, kind),
        out_shape=(VMEM((cols, LANES), F32), jax.ShapeDtypeStruct((1, rows), F32)),
        in_specs=full(3 + len(more)),
        out_specs=tuple(full(2)),
        compiler_params=params(),
        name="sweep_" + kind,
    )(q, b, *more, w)


def finish_kernel(total_cols, q_ref, x_ref, y_ref, b_ref, sq_ref, beta_ref, bv2_ref, bv3_ref,
                  mid_ref, gb1_ref, vb_ref, rows_ref, pot_ref, arch_ref, new_ref, half_ref, tr_ref):
    cols, rows = q_ref.shape
    width = y_ref.shape[1]
    step = 256
    for jb in range(cols // step):
        def body(g, carry):
            base = pl.multiple_of(g * 2 * SUB, 2 * SUB)
            parts = []
            for h in range(2):
                s = pl.ds(jb * step + base + h * SUB, SUB)
                b, bv2, bv3 = b_ref[s, :], bv2_ref[s, :], bv3_ref[s, :]
                mid, gb1, vb = mid_ref[s, :], gb1_ref[s, :], vb_ref[s, :]
                outs, dots = [], []
                for l in range(rows // LANES):
                    ls = pl.ds(l * LANES, LANES)
                    q = q_ref[s, ls]
                    r = [wide(rows_ref[pl.ds(i, 1), ls]) for i in range(5)]
                    c = r[0] * bv3 + r[1] * bv2 + r[2] * mid + r[3] * b + r[4] * vb + gb1
                    outs.append(q * c)
                    dots.append(q * r[4])
                gb0 = vb * lane_sum(dots)
                tr_ref[s, :] = b + 2.0 * (mid * b / bv2 + gb1) + gb0
                parts.append(outs)
            for l in range(rows // LANES):
                half_ref[pl.ds(base, 2 * SUB), pl.ds(l * LANES, LANES)] = jnp.concatenate(
                    [parts[0][l], parts[1][l]], axis=0).astype(BF16)
            return carry

        lax.fori_loop(0, step // (2 * SUB), body, 0)
        js = pl.ds(jb * step, step)
        y = y_ref[js, :]
        back = jnp.dot(half_ref[...], x_ref[...], preferred_element_type=F32)
        tr = tr_ref[js, :]
        for l in range(width // LANES):
            ls = slice(l * LANES, (l + 1) * LANES)
            arch_ref[js, ls] = total_cols * (tr * y[:, ls].astype(F32) - back[:, ls])
        prod = lax.dot_general(half_ref[...], y, (((0,), (0,)), ((), ())), preferred_element_type=F32)
        new_ref[...] = prod if jb == 0 else new_ref[...] + prod
    for c in range(cols // LANES):
        s = pl.ds(c * LANES, LANES)
        pot = (beta_ref[s, :] + sq_ref[s, :] + jnp.log2(bv3_ref[s, :] / b_ref[s, :])) * (1.0 / LOGK)
        pot_ref[:, s] = jnp.transpose(pot)[0:1, :]


def finish(total_cols, q, x, y, *rest):
    cols, rows = q.shape
    width = y.shape[1]
    return pl.pallas_call(
        functools.partial(finish_kernel, float(total_cols)),
        out_shape=(
            jax.ShapeDtypeStruct((1, cols), F32),
            jax.ShapeDtypeStruct((cols, width), F32),
            jax.ShapeDtypeStruct((rows, width), F32),
        ),
        in_specs=full(3 + len(rest)),
        out_specs=tuple(full(3)),
        scratch_shapes=[pltpu.VMEM((256, rows), BF16), pltpu.VMEM((cols, LANES), F32)],
        compiler_params=params(),
        name="finish",
    )(q, x, y, *rest)


def combine(x, count, join):
    def swap(v, k):
        return lax.ppermute(v, "cols", [(i, i ^ k) for i in range(count)])

    k = 1
    while k < count:
        if 4 * k <= count:
            x = join([x, swap(x, k), swap(x, 2 * k), swap(x, 3 * k)])
            k *= 4
        else:
            x = join([x, swap(x, k)])
            k *= 2
    return x


def add_join(xs):
    return tree(jnp.add, xs)


def lse_join(xs):
    m = tree(jnp.maximum, xs)
    return m + jnp.log2(tree(jnp.add, [jnp.exp2(x - m) for x in xs]))


def local(new_points, arch_points, new_mass, arch_mass):
    rows = new_points.shape[0]
    count = lax.axis_size("cols")
    if count & (count - 1):
        def reduce_add(x):
            return lax.psum(x, "cols")

        def reduce_lse(x):
            m = lax.pmax(x, "cols")
            return m + jnp.log2(lax.psum(jnp.exp2(x - m), "cols"))
    else:
        reduce_add = functools.partial(combine, count=count, join=add_join)
        reduce_lse = functools.partial(combine, count=count, join=lse_join)
    total_cols = arch_points.shape[0] * count
    width = new_points.shape[1]
    new_float = new_points.astype(F32)
    sq_new = jnp.sum(new_float * new_float, 1) * (LOGK / width)
    a = (new_mass / rows).reshape(1, rows)

    z, b, sq, lse = scores(new_points, arch_points, arch_mass, total_cols)
    alpha = -reduce_lse(lse)
    q, beta, vb, part = plan(z, b, sq, jnp.log2(a) + alpha)
    u2 = a / reduce_add(part)
    bv2, part = sweep("fwd", q, b, u2)
    u3 = a / reduce_add(part)
    bv3, part = sweep("fwd", q, b, u3)
    fbar3 = a + u3 * reduce_add(part)
    w3 = u3 * fbar3 / a
    mid, part = sweep("mid", q, b, w3, bv2 / b)
    fbar2 = u2 * reduce_add(part)
    w2 = u2 * fbar2 / a
    gb1, part = sweep("bwd", q, b, w2)
    fbar1 = reduce_add(part)
    w1 = fbar1 / a
    packed = jnp.concatenate([u3, w3, u2, w2, w1], axis=0)
    pot, arch_grad, product = finish(
        total_cols, q, new_points, arch_points, b, sq, beta, bv2, bv3, mid, gb1, vb, packed
    )
    share = rows // count
    start = lax.axis_index("cols") * share
    summed = lax.psum_scatter(product, "cols", scatter_dimension=0, tiled=True)
    row_weight = 2.0 * (fbar3 + fbar2 + fbar1) - a
    mine = lax.dynamic_slice_in_dim(row_weight.reshape(rows), start, share, 0)
    points = lax.dynamic_slice_in_dim(new_points, start, share, 0).astype(F32)
    new_grad = rows * (mine[:, None] * points - summed)
    new_pot = (alpha.reshape(rows) + jnp.log2(u3).reshape(rows) + sq_new) * (1.0 / LOGK)
    return (new_pot, pot.reshape(-1), new_grad, arch_grad)


def solution(mesh):
    in_specs = (P("pairs", None), P(("pairs", "cols"), None), P("pairs"), P(("pairs", "cols")))
    out_specs = (
        P("pairs"),
        P(("pairs", "cols")),
        P(("pairs", "cols"), None),
        P(("pairs", "cols"), None),
    )
    return jax.shard_map(local, mesh=mesh, in_specs=in_specs, out_specs=out_specs, check_vma=False)
```

```python
import functools
import math
import jax
import jax.numpy as jnp
from jax import lax
from jax.experimental import pallas as pl
from jax.experimental.pallas import tpu as pltpu
from jax.sharding import PartitionSpec as P

EPSILON = 0.05
LOGK = math.log2(math.e) / EPSILON
LANES = 128
SUB = 8
VMEM = pltpu.VMEM
F32 = jnp.float32
BF16 = jnp.bfloat16


def params(mib=28):
    return pltpu.CompilerParams(vmem_limit_bytes=mib * 1024 * 1024)


def full(n):
    return [pl.BlockSpec(memory_space=VMEM)] * n


def column(row):
    return jnp.transpose(jnp.broadcast_to(row, (LANES, LANES)))


def lanes(x):
    return [x[:, l * LANES:(l + 1) * LANES] for l in range(x.shape[1] // LANES)]


def wide(x):
    return jnp.broadcast_to(x, (SUB, LANES))


def tree(op, xs):
    xs = list(xs)
    while len(xs) > 1:
        xs = [op(xs[i], xs[i + 1]) if i + 1 < len(xs) else xs[i] for i in range(0, len(xs), 2)]
    return xs[0]


def lane_sum(xs):
    return wide(jnp.sum(tree(jnp.add, xs), axis=1, keepdims=True))


def lane_max(xs):
    return wide(jnp.max(tree(jnp.maximum, xs), axis=1, keepdims=True))


def rows_of(i, n):
    return pl.ds(pl.multiple_of(i * n, n), n)


def scores_kernel(total_cols, x_ref, y_ref, mass_ref, z_ref, b_ref, sq_ref, lse_ref, cb_ref):
    cols, width = y_ref.shape
    rows = x_ref.shape[0]
    for c in range(cols // LANES):
        s = pl.ds(c * LANES, LANES)
        b = column(mass_ref[:, s] * (1.0 / total_cols))
        b_ref[s, :] = b
        yf = y_ref[s, :].astype(F32)
        sq = jnp.sum(yf * yf, axis=1, keepdims=True) * (LOGK / width)
        sq = jnp.broadcast_to(sq, (LANES, LANES))
        sq_ref[s, :] = sq
        cb_ref[s, :] = jnp.log2(b) - sq
    step = 2 * LANES
    many = 4

    def reduce_block(r):
        for l in range(step // LANES):
            ls = pl.ds(r * step + l * LANES, LANES)
            m = [None] * many
            for g in range(cols // SUB):
                s = pl.ds(g * SUB, SUB)
                v = z_ref[s, ls] + cb_ref[s, :]
                m[g % many] = v if m[g % many] is None else jnp.maximum(m[g % many], v)
            m = jnp.max(tree(jnp.maximum, m), axis=0, keepdims=True)
            mw = wide(m)
            t = [None] * many
            for g in range(cols // SUB):
                s = pl.ds(g * SUB, SUB)
                v = jnp.exp2(z_ref[s, ls] + cb_ref[s, :] - mw)
                t[g % many] = v if t[g % many] is None else t[g % many] + v
            lse_ref[:, ls] = m + jnp.log2(jnp.sum(tree(jnp.add, t), axis=0, keepdims=True))

    for r in range(rows // step):
        s = pl.ds(r * step, step)
        z_ref[:, s] = lax.dot_general(
            y_ref[...], x_ref[s, :], (((1,), (1,)), ((), ())), preferred_element_type=F32
        ) * (2.0 * LOGK / width)
        if r > 0:
            reduce_block(r - 1)
    reduce_block(rows // step - 1)


def scores(new_points, arch_points, arch_mass, total_cols):
    rows, cols = new_points.shape[0], arch_points.shape[0]
    return pl.pallas_call(
        functools.partial(scores_kernel, total_cols),
        out_shape=(
            VMEM((cols, rows), F32),
            VMEM((cols, LANES), F32),
            VMEM((cols, LANES), F32),
            jax.ShapeDtypeStruct((1, rows), F32),
        ),
        in_specs=full(3),
        out_specs=tuple(full(4)),
        scratch_shapes=[pltpu.VMEM((cols, LANES), F32)],
        compiler_params=params(),
        name="scores",
    )(new_points, arch_points, arch_mass.reshape(1, cols))


CHUNK = 128


def groups(i):
    return [pl.ds(pl.multiple_of(i * CHUNK, CHUNK) + h * SUB, SUB) for h in range(CHUNK // SUB)]


def column_dots(e_ref, w, tmp_ref):
    def body(i, carry):
        for s in groups(i):
            tmp_ref[s, :] = tree(jnp.add, [a * c for a, c in zip(lanes(e_ref[s, :]), w)])
        return carry

    lax.fori_loop(0, e_ref.shape[0] // CHUNK, body, 0)


def row_sums(e_ref, c_ref, part_ref):
    def body(i, acc):
        for s in groups(i):
            c = c_ref[s, :]
            acc = [a + d * c for a, d in zip(acc, lanes(e_ref[s, :]))]
        return acc

    cols, rows = e_ref.shape
    acc = lax.fori_loop(0, cols // CHUNK, body, [jnp.zeros((SUB, LANES), F32)] * (rows // LANES))
    for l, a in enumerate(acc):
        part_ref[:, pl.ds(l * LANES, LANES)] = jnp.sum(a, axis=0, keepdims=True)


def spread(x, op):
    return jnp.broadcast_to(op(x, axis=1, keepdims=True), x.shape)


def plan_kernel(z_ref, b_ref, sq_ref, w_ref, e_ref, n_ref, r_ref, br_ref, vbr_ref, part_ref, tmp_ref):
    cols, rows = z_ref.shape
    w = [wide(a) for a in lanes(w_ref[...])]

    def top(i, carry):
        for s in groups(i):
            tmp_ref[s, :] = tree(jnp.maximum, [a + c for a, c in zip(lanes(z_ref[s, :]), w)])
        return carry

    lax.fori_loop(0, cols // CHUNK, top, 0)

    def spread_top(i, carry):
        s = rows_of(i, CHUNK)
        n_ref[s, :] = spread(tmp_ref[s, :], jnp.max)
        return carry

    lax.fori_loop(0, cols // CHUNK, spread_top, 0)

    def powers(i, carry):
        for s in groups(i):
            n = n_ref[s, :]
            e = [jnp.exp2(a + c - n) for a, c in zip(lanes(z_ref[s, :]), w)]
            for l, a in enumerate(e):
                e_ref[s, pl.ds(l * LANES, LANES)] = a
            tmp_ref[s, :] = tree(jnp.add, e)
        return carry

    lax.fori_loop(0, cols // CHUNK, powers, 0)

    def scale(i, carry):
        s = rows_of(i, CHUNK)
        t = spread(tmp_ref[s, :], jnp.sum)
        r = 1.0 / t
        br = b_ref[s, :] * r
        r_ref[s, :] = r
        br_ref[s, :] = br
        vbr_ref[s, :] = br * jnp.exp2(n_ref[s, :] + jnp.log2(t) - sq_ref[s, :])
        return carry

    lax.fori_loop(0, cols // CHUNK, scale, 0)
    row_sums(e_ref, br_ref, part_ref)


def plan(z, b, sq, w):
    cols, rows = z.shape
    return pl.pallas_call(
        plan_kernel,
        out_shape=(VMEM((cols, rows), F32),) + (VMEM((cols, LANES), F32),) * 4
        + (jax.ShapeDtypeStruct((1, rows), F32),),
        in_specs=full(4),
        out_specs=tuple(full(6)),
        scratch_shapes=[pltpu.VMEM((cols, LANES), F32)],
        input_output_aliases={0: 0},
        compiler_params=params(8),
        name="plan",
    )(z, b, sq, w)


def sweep_kernel(kind, e_ref, b_ref, *refs):
    cols, rows = e_ref.shape
    more = refs[:-4]
    w_ref, c_ref, part_ref, tmp_ref = refs[-4:]
    column_dots(e_ref, [wide(a) for a in lanes(w_ref[...])], tmp_ref)

    def weigh(i, carry):
        s = rows_of(i, CHUNK)
        t = spread(tmp_ref[s, :], jnp.sum)
        b = b_ref[s, :]
        if kind == "fwd":
            c = b / t
        elif kind == "mid":
            v = more[0][s, :]
            c = v * v * t / b
        else:
            c = b * t * more[0][s, :]
        c_ref[s, :] = c
        return carry

    lax.fori_loop(0, cols // CHUNK, weigh, 0)
    row_sums(e_ref, c_ref, part_ref)


def sweep(kind, e, b, *more):
    cols, rows = e.shape
    return pl.pallas_call(
        functools.partial(sweep_kernel, kind),
        out_shape=(VMEM((cols, LANES), F32), jax.ShapeDtypeStruct((1, rows), F32)),
        in_specs=full(2 + len(more)),
        out_specs=tuple(full(2)),
        scratch_shapes=[pltpu.VMEM((cols, LANES), F32)],
        compiler_params=params(8),
        name="sweep_" + kind,
    )(e, b, *more)


def mix_kernel(share, pieces, me_ref, e_ref, y_ref, *refs):
    c_refs, r_refs = refs[:6], refs[6:11]
    half_ref, keep_ref = refs[11:13]
    send_refs, prod_ref = refs[13:-1], refs[-1]
    cols, rows = e_ref.shape
    pair = 2 * share
    me = me_ref[0]
    core = me % 2
    for p in range(rows // pair):
        lo = pl.multiple_of(((me // 2) ^ p) * pair, pair)
        spots = [pl.ds(pl.multiple_of(lo + l * LANES, LANES), LANES) for l in range(pair // LANES)]
        r = [[wide(ref[:, ls]) for ref in r_refs] for ls in spots]
        for g in range(cols // (2 * SUB)):
            outs = [[] for _ in spots]
            for h in range(2):
                s = pl.ds(g * 2 * SUB + h * SUB, SUB)
                c = [ref[s, :] for ref in c_refs]
                for o, rl, ls in zip(outs, r, spots):
                    terms = [a * b for a, b in zip(c, rl)] + [c[5]]
                    o.append(e_ref[s, ls] * tree(jnp.add, terms))
            for o, ls in zip(outs, spots):
                half_ref[pl.ds(g * 2 * SUB, 2 * SUB), ls] = jnp.concatenate(o, axis=0).astype(BF16)
        prod_ref[p % 2] = lax.dot_general(
            half_ref[:, pl.ds(lo, pair)], y_ref[...], (((0,), (0,)), ((), ())),
            preferred_element_type=F32,
        )
        keep_ref[p] = prod_ref[p % 2, pl.ds(pl.multiple_of(core * share, share), share), :]
        at = (1 - core) * share
        for ref, n in zip(send_refs, pieces):
            ref[p] = prod_ref[p % 2, pl.ds(pl.multiple_of(at, 8), n), :]
            at = at + n


def mix(share, pieces, me, e, y, columns, weights):
    cols, rows = e.shape
    width = y.shape[1]
    pairs = rows // (2 * share)
    out = [VMEM((cols, rows), BF16), jax.ShapeDtypeStruct((pairs, share, width), F32)]
    out += [jax.ShapeDtypeStruct((pairs, n, width), F32) for n in pieces]
    got = pl.pallas_call(
        functools.partial(mix_kernel, share, pieces),
        out_shape=tuple(out),
        in_specs=[pl.BlockSpec(memory_space=pltpu.SMEM)] + full(13),
        out_specs=tuple(full(len(out))),
        scratch_shapes=[pltpu.VMEM((2, 2 * share, width), F32)],
        compiler_params=params(16),
        name="mix",
    )(me.reshape(1), e, y, *columns, *weights)
    return got[0], got[1], got[2:]


def back_kernel(total_cols, half_ref, x_ref, y_ref, e_ref, b_ref, r_ref, n_ref, sq_ref, bv2_ref,
                bv3_ref, mid_ref, gb1_ref, vbr_ref, w_ref, pot_ref, arch_ref, tmp_ref):
    cols, rows = e_ref.shape
    width = y_ref.shape[1]
    column_dots(e_ref, [wide(a) for a in lanes(w_ref[...])], tmp_ref)
    step = 256
    for j in range(cols // step):
        s = pl.ds(j * step, step)
        b = b_ref[s, :]
        gb0 = vbr_ref[s, :] * spread(tmp_ref[s, :], jnp.sum)
        gb2 = mid_ref[s, :] * b / bv2_ref[s, :]
        tr = b + 2.0 * (gb2 + gb1_ref[s, :] / r_ref[s, :]) + gb0
        back = jnp.dot(half_ref[s, :], x_ref[...], preferred_element_type=F32)
        for l in range(width // LANES):
            ls = slice(l * LANES, (l + 1) * LANES)
            arch_ref[s, ls] = total_cols * (tr * y_ref[s, ls].astype(F32) - back[:, ls])
    for c in range(cols // LANES):
        s = pl.ds(c * LANES, LANES)
        pot = (sq_ref[s, :] - n_ref[s, :] + jnp.log2(bv3_ref[s, :] / b_ref[s, :])) * (1.0 / LOGK)
        pot_ref[:, s] = jnp.transpose(pot)[0:1, :]


def back(total_cols, half, x, y, *rest):
    cols, rows = half.shape
    width = y.shape[1]
    return pl.pallas_call(
        functools.partial(back_kernel, float(total_cols)),
        out_shape=(
            jax.ShapeDtypeStruct((1, cols), F32),
            jax.ShapeDtypeStruct((cols, width), F32),
        ),
        in_specs=full(3 + len(rest)),
        out_specs=tuple(full(2)),
        scratch_shapes=[pltpu.VMEM((cols, LANES), F32)],
        compiler_params=params(16),
        cost_estimate=pl.CostEstimate(
            flops=2 * cols * rows * width, bytes_accessed=16 * 1024 * 1024, transcendentals=0
        ),
        name="back",
    )(half, x, y, *rest)


def swap(v, k, count):
    return lax.ppermute(v, "cols", [(i, i ^ k) for i in range(count)])


def scatter_sum(keep, sends, pieces, count):
    bits = [1 << i for i in range(1, count.bit_length() - 1)]
    done, at = [], 0
    for i, (send, n) in enumerate(zip(sends, pieces)):
        got = swap(send, 1, count)
        v = {p: keep[p, at:at + n] + got[p] for p in range(count // 2)}
        at += n
        order = bits if i < (len(pieces) + 1) // 2 else bits[1:] + bits[:1]
        for k in order:
            away = [p for p in sorted(v) if p & (k // 2)]
            got = swap(jnp.concatenate([v[p] for p in away], axis=0), k, count)
            v = {p ^ (k // 2): v[p ^ (k // 2)] + got[j * n:(j + 1) * n] for j, p in enumerate(away)}
        done.append(v[0])
    return jnp.concatenate(done, axis=0)


def combine(x, count, join):
    k = 1
    while k < count:
        if 4 * k <= count:
            x = join([x] + [swap(x, j * k, count) for j in (1, 2, 3)])
            k *= 4
        else:
            x = join([x, swap(x, k, count)])
            k *= 2
    return x


def add_join(xs):
    return tree(jnp.add, xs)


def lse_join(xs):
    m = tree(jnp.maximum, xs)
    return m + jnp.log2(tree(jnp.add, [jnp.exp2(x - m) for x in xs]))


def local(new_points, arch_points, new_mass, arch_mass):
    rows, width = new_points.shape
    count = lax.axis_size("cols")
    assert count & (count - 1) == 0
    reduce_add = functools.partial(combine, count=count, join=add_join)
    reduce_lse = functools.partial(combine, count=count, join=lse_join)
    total_cols = arch_points.shape[0] * count
    share = rows // count
    me = lax.axis_index("cols")
    new_float = new_points.astype(F32)
    sq_new = jnp.sum(new_float * new_float, 1) * (LOGK / width)
    a = (new_mass / rows).reshape(1, rows)

    z, b, sq, lse = scores(new_points, arch_points, arch_mass, total_cols)
    alpha = -reduce_lse(lse)
    e, n, r, br, vbr, part = plan(z, b, sq, jnp.log2(a) + alpha)
    u2 = a / reduce_add(part)
    bv2, part = sweep("fwd", e, b, u2)
    u3 = a / reduce_add(part)
    bv3, part = sweep("fwd", e, b, u3)
    fbar3 = a + u3 * reduce_add(part)
    w3 = u3 * fbar3 / a
    mid, part = sweep("mid", e, b, bv2, w3)
    fbar2 = u2 * reduce_add(part)
    w2 = u2 * fbar2 / a
    gb1, part = sweep("bwd", e, br, r, w2)
    fbar1 = reduce_add(part)
    w1 = fbar1 / a
    pieces = [share * f // 16 for f in (6, 6, 4)]
    half, keep, sends = mix(
        share, pieces, me, e, arch_points, (bv3, bv2, mid, br, vbr, gb1), (u3, w3, u2, w2, w1)
    )
    pot, arch_grad = back(
        total_cols, half, new_points, arch_points, e, b, r, n, sq, bv2, bv3, mid, gb1, vbr, w1
    )
    summed = scatter_sum(keep, sends, pieces, count)
    row_weight = 2.0 * (fbar3 + fbar2 + fbar1) - a
    mine = lax.dynamic_slice_in_dim(row_weight.reshape(rows), me * share, share, 0)
    points = lax.dynamic_slice_in_dim(new_points, me * share, share, 0).astype(F32)
    new_grad = rows * (mine[:, None] * points - summed)
    new_pot = (alpha.reshape(rows) + jnp.log2(u3).reshape(rows) + sq_new) * (1.0 / LOGK)
    return (new_pot, pot.reshape(-1), new_grad, arch_grad)


def solution(mesh):
    in_specs = (P("pairs", None), P(("pairs", "cols"), None), P("pairs"), P(("pairs", "cols")))
    out_specs = (
        P("pairs"),
        P(("pairs", "cols")),
        P(("pairs", "cols"), None),
        P(("pairs", "cols"), None),
    )
    return jax.shard_map(local, mesh=mesh, in_specs=in_specs, out_specs=out_specs, check_vma=False)
```

```python
import functools
import math
import jax
import jax.numpy as jnp
from jax import lax
from jax.experimental import pallas as pl
from jax.experimental.pallas import tpu as pltpu
from jax.sharding import PartitionSpec as P

EPSILON = 0.05
LOGK = math.log2(math.e) / EPSILON
LANES = 128
SUB = 8
VMEM = pltpu.VMEM
F32 = jnp.float32
BF16 = jnp.bfloat16


def params(mib=28):
    return pltpu.CompilerParams(vmem_limit_bytes=mib * 1024 * 1024)


def full(n):
    return [pl.BlockSpec(memory_space=VMEM)] * n


def column(row):
    return jnp.transpose(jnp.broadcast_to(row, (LANES, LANES)))


def lanes(x):
    return [x[:, l * LANES:(l + 1) * LANES] for l in range(x.shape[1] // LANES)]


def wide(x):
    return jnp.broadcast_to(x, (SUB, LANES))


def tree(op, xs):
    xs = list(xs)
    while len(xs) > 1:
        xs = [op(xs[i], xs[i + 1]) if i + 1 < len(xs) else xs[i] for i in range(0, len(xs), 2)]
    return xs[0]


def lane_sum(xs):
    return wide(jnp.sum(tree(jnp.add, xs), axis=1, keepdims=True))


def lane_max(xs):
    return wide(jnp.max(tree(jnp.maximum, xs), axis=1, keepdims=True))


def rows_of(i, n):
    return pl.ds(pl.multiple_of(i * n, n), n)


def scores_kernel(total_cols, share, x_ref, y_ref, mass_ref, z_ref, b_ref, sq_ref, lse_ref, mine_ref,
                  cb_ref):
    cols, width = y_ref.shape
    rows = x_ref.shape[0]
    first = pl.multiple_of(lax.axis_index("cols") * share, share)
    mine_ref[...] = x_ref[pl.ds(first, share), :].astype(F32)
    for c in range(cols // LANES):
        s = pl.ds(c * LANES, LANES)
        b = column(mass_ref[:, s] * (1.0 / total_cols))
        b_ref[s, :] = b
        yf = y_ref[s, :].astype(F32)
        sq = jnp.sum(yf * yf, axis=1, keepdims=True) * (LOGK / width)
        sq = jnp.broadcast_to(sq, (LANES, LANES))
        sq_ref[s, :] = sq
        cb_ref[s, :] = jnp.log2(b) - sq
    step = 2 * LANES
    many = 4

    def reduce_block(r):
        for l in range(step // LANES):
            ls = pl.ds(r * step + l * LANES, LANES)
            m = [None] * many
            for g in range(cols // SUB):
                s = pl.ds(g * SUB, SUB)
                v = z_ref[s, ls] + cb_ref[s, :]
                m[g % many] = v if m[g % many] is None else jnp.maximum(m[g % many], v)
            m = jnp.max(tree(jnp.maximum, m), axis=0, keepdims=True)
            mw = wide(m)
            t = [None] * many
            for g in range(cols // SUB):
                s = pl.ds(g * SUB, SUB)
                v = jnp.exp2(z_ref[s, ls] + cb_ref[s, :] - mw)
                t[g % many] = v if t[g % many] is None else t[g % many] + v
            lse_ref[:, ls] = m + jnp.log2(jnp.sum(tree(jnp.add, t), axis=0, keepdims=True))

    for r in range(rows // step):
        s = pl.ds(r * step, step)
        z_ref[:, s] = lax.dot_general(
            y_ref[...], x_ref[s, :], (((1,), (1,)), ((), ())), preferred_element_type=F32
        ) * (2.0 * LOGK / width)
        if r > 0:
            reduce_block(r - 1)
    reduce_block(rows // step - 1)


def scores(new_points, arch_points, arch_mass, total_cols, share):
    rows, cols = new_points.shape[0], arch_points.shape[0]
    return pl.pallas_call(
        functools.partial(scores_kernel, total_cols, share),
        out_shape=(
            VMEM((cols, rows), F32),
            VMEM((cols, LANES), F32),
            VMEM((cols, LANES), F32),
            jax.ShapeDtypeStruct((1, rows), F32),
            VMEM((share, new_points.shape[1]), F32),
        ),
        in_specs=full(3),
        out_specs=tuple(full(5)),
        scratch_shapes=[pltpu.VMEM((cols, LANES), F32)],
        compiler_params=params(),
        name="scores",
    )(new_points, arch_points, arch_mass.reshape(1, cols))


CHUNK = 128


def groups(i):
    return [pl.ds(pl.multiple_of(i * CHUNK, CHUNK) + h * SUB, SUB) for h in range(CHUNK // SUB)]


def column_dots(e_ref, w, tmp_ref):
    def body(i, carry):
        for s in groups(i):
            tmp_ref[s, :] = tree(jnp.add, [a * c for a, c in zip(lanes(e_ref[s, :]), w)])
        return carry

    lax.fori_loop(0, e_ref.shape[0] // CHUNK, body, 0)


def row_sums(e_ref, c_ref, part_ref):
    def body(i, acc):
        for s in groups(i):
            c = c_ref[s, :]
            acc = [a + d * c for a, d in zip(acc, lanes(e_ref[s, :]))]
        return acc

    cols, rows = e_ref.shape
    acc = lax.fori_loop(0, cols // CHUNK, body, [jnp.zeros((SUB, LANES), F32)] * (rows // LANES))
    for l, a in enumerate(acc):
        part_ref[:, pl.ds(l * LANES, LANES)] = jnp.sum(a, axis=0, keepdims=True)


def spread(x, op):
    return jnp.broadcast_to(op(x, axis=1, keepdims=True), x.shape)


def plan_kernel(z_ref, b_ref, sq_ref, w_ref, e_ref, n_ref, r_ref, br_ref, vbr_ref, part_ref, tmp_ref):
    cols, rows = z_ref.shape
    w = [wide(a) for a in lanes(w_ref[...])]

    def top(i, carry):
        for s in groups(i):
            tmp_ref[s, :] = tree(jnp.maximum, [a + c for a, c in zip(lanes(z_ref[s, :]), w)])
        return carry

    lax.fori_loop(0, cols // CHUNK, top, 0)

    def spread_top(i, carry):
        s = rows_of(i, CHUNK)
        n_ref[s, :] = spread(tmp_ref[s, :], jnp.max)
        return carry

    lax.fori_loop(0, cols // CHUNK, spread_top, 0)

    def powers(i, carry):
        for s in groups(i):
            n = n_ref[s, :]
            e = [jnp.exp2(a + c - n) for a, c in zip(lanes(z_ref[s, :]), w)]
            for l, a in enumerate(e):
                e_ref[s, pl.ds(l * LANES, LANES)] = a
            tmp_ref[s, :] = tree(jnp.add, e)
        return carry

    lax.fori_loop(0, cols // CHUNK, powers, 0)

    def scale(i, carry):
        s = rows_of(i, CHUNK)
        t = spread(tmp_ref[s, :], jnp.sum)
        r = 1.0 / t
        br = b_ref[s, :] * r
        r_ref[s, :] = r
        br_ref[s, :] = br
        vbr_ref[s, :] = br * jnp.exp2(n_ref[s, :] + jnp.log2(t) - sq_ref[s, :])
        return carry

    lax.fori_loop(0, cols // CHUNK, scale, 0)
    row_sums(e_ref, br_ref, part_ref)


def plan(z, b, sq, w):
    cols, rows = z.shape
    return pl.pallas_call(
        plan_kernel,
        out_shape=(VMEM((cols, rows), F32),) + (VMEM((cols, LANES), F32),) * 4
        + (jax.ShapeDtypeStruct((1, rows), F32),),
        in_specs=full(4),
        out_specs=tuple(full(6)),
        scratch_shapes=[pltpu.VMEM((cols, LANES), F32)],
        input_output_aliases={0: 0},
        compiler_params=params(8),
        name="plan",
    )(z, b, sq, w)


def sweep_kernel(kind, e_ref, b_ref, *refs):
    cols, rows = e_ref.shape
    more = refs[:-4]
    w_ref, c_ref, part_ref, tmp_ref = refs[-4:]
    column_dots(e_ref, [wide(a) for a in lanes(w_ref[...])], tmp_ref)

    def weigh(i, carry):
        s = rows_of(i, CHUNK)
        t = spread(tmp_ref[s, :], jnp.sum)
        b = b_ref[s, :]
        if kind == "fwd":
            c = b / t
        elif kind == "mid":
            v = more[0][s, :]
            c = v * v * t / b
        else:
            c = b * t * more[0][s, :]
        c_ref[s, :] = c
        return carry

    lax.fori_loop(0, cols // CHUNK, weigh, 0)
    row_sums(e_ref, c_ref, part_ref)


def sweep(kind, e, b, *more):
    cols, rows = e.shape
    return pl.pallas_call(
        functools.partial(sweep_kernel, kind),
        out_shape=(VMEM((cols, LANES), F32), jax.ShapeDtypeStruct((1, rows), F32)),
        in_specs=full(2 + len(more)),
        out_specs=tuple(full(2)),
        scratch_shapes=[pltpu.VMEM((cols, LANES), F32)],
        compiler_params=params(8),
        name="sweep_" + kind,
    )(e, b, *more)


def mix_kernel(share, pieces, e_ref, y_ref, *refs):
    c_refs, r_refs = refs[:6], refs[6:11]
    half_ref, keep_ref = refs[11:13]
    send_refs, prod_ref = refs[13:-1], refs[-1]
    cols, rows = e_ref.shape
    pair = 2 * share
    me = lax.axis_index("cols")
    core = me % 2
    for p in range(rows // pair):
        lo = pl.multiple_of(((me // 2) ^ p) * pair, pair)
        spots = [pl.ds(pl.multiple_of(lo + l * LANES, LANES), LANES) for l in range(pair // LANES)]
        r = [[wide(ref[:, ls]) for ref in r_refs] for ls in spots]
        for g in range(cols // (2 * SUB)):
            outs = [[] for _ in spots]
            for h in range(2):
                s = pl.ds(g * 2 * SUB + h * SUB, SUB)
                c = [ref[s, :] for ref in c_refs]
                for o, rl, ls in zip(outs, r, spots):
                    terms = [a * b for a, b in zip(c, rl)] + [c[5]]
                    o.append(e_ref[s, ls] * tree(jnp.add, terms))
            for o, ls in zip(outs, spots):
                half_ref[pl.ds(g * 2 * SUB, 2 * SUB), ls] = jnp.concatenate(o, axis=0).astype(BF16)
        prod_ref[p % 2] = lax.dot_general(
            half_ref[:, pl.ds(lo, pair)], y_ref[...], (((0,), (0,)), ((), ())),
            preferred_element_type=F32,
        )
        keep_ref[p] = prod_ref[p % 2, pl.ds(pl.multiple_of(core * share, share), share), :]
        at = (1 - core) * share
        for ref, n in zip(send_refs, pieces):
            ref[p] = prod_ref[p % 2, pl.ds(pl.multiple_of(at, 8), n), :]
            at = at + n


def mix(share, pieces, e, y, columns, weights):
    cols, rows = e.shape
    width = y.shape[1]
    pairs = rows // (2 * share)
    out = [VMEM((cols, rows), BF16), jax.ShapeDtypeStruct((pairs, share, width), F32)]
    out += [jax.ShapeDtypeStruct((pairs, n, width), F32) for n in pieces]
    got = pl.pallas_call(
        functools.partial(mix_kernel, share, pieces),
        out_shape=tuple(out),
        in_specs=full(13),
        out_specs=tuple(full(len(out))),
        scratch_shapes=[pltpu.VMEM((2, 2 * share, width), F32)],
        compiler_params=params(16),
        name="mix",
    )(e, y, *columns, *weights)
    return got[0], got[1], got[2:]


def back_kernel(total_cols, half_ref, x_ref, y_ref, e_ref, b_ref, r_ref, n_ref, sq_ref, bv2_ref,
                bv3_ref, mid_ref, gb1_ref, vbr_ref, w_ref, alpha_ref, u3_ref, after_ref, pot_ref, arch_ref,
                new_ref, tmp_ref):
    del after_ref
    cols, rows = e_ref.shape
    width = y_ref.shape[1]
    column_dots(e_ref, [wide(a) for a in lanes(w_ref[...])], tmp_ref)
    step = 256
    for j in range(cols // step):
        s = pl.ds(j * step, step)
        b = b_ref[s, :]
        gb0 = vbr_ref[s, :] * spread(tmp_ref[s, :], jnp.sum)
        gb2 = mid_ref[s, :] * b / bv2_ref[s, :]
        tr = b + 2.0 * (gb2 + gb1_ref[s, :] / r_ref[s, :]) + gb0
        back = jnp.dot(half_ref[s, :], x_ref[...], preferred_element_type=F32)
        for l in range(width // LANES):
            ls = slice(l * LANES, (l + 1) * LANES)
            arch_ref[s, ls] = total_cols * (tr * y_ref[s, ls].astype(F32) - back[:, ls])
    for c in range(cols // LANES):
        s = pl.ds(c * LANES, LANES)
        pot = (sq_ref[s, :] - n_ref[s, :] + jnp.log2(bv3_ref[s, :] / b_ref[s, :])) * (1.0 / LOGK)
        pot_ref[:, s] = jnp.transpose(pot)[0:1, :]
    ones = jnp.ones((SUB, width), BF16)
    for i in range(rows // step):
        s = pl.ds(i * step, step)
        xf = x_ref[s, :].astype(F32)
        square = xf * xf
        high = square.astype(BF16)
        low = (square - high.astype(F32)).astype(BF16)
        sq = sum(
            lax.dot_general(ones, v, (((1,), (1,)), ((), ())), preferred_element_type=F32)
            for v in (high, low)
        )[0:1, :] * (LOGK / width)
        new_ref[:, s] = (alpha_ref[:, s] + jnp.log2(u3_ref[:, s]) + sq) * (1.0 / LOGK)


def back(total_cols, half, x, y, *rest):
    cols, rows = half.shape
    width = y.shape[1]
    return pl.pallas_call(
        functools.partial(back_kernel, float(total_cols)),
        out_shape=(
            jax.ShapeDtypeStruct((1, cols), F32),
            jax.ShapeDtypeStruct((cols, width), F32),
            jax.ShapeDtypeStruct((1, rows), F32),
        ),
        in_specs=full(2 + len(rest)) + [pl.BlockSpec(memory_space=pl.ANY)],
        out_specs=tuple(full(3)),
        scratch_shapes=[pltpu.VMEM((cols, LANES), F32)],
        compiler_params=params(16),
        cost_estimate=pl.CostEstimate(
            flops=2 * cols * rows * width, bytes_accessed=16 * 1024 * 1024, transcendentals=0
        ),
        name="back",
    )(half, x, y, *rest)


def swap(v, k, count):
    return lax.ppermute(v, "cols", [(i, i ^ k) for i in range(count)])


def scatter_sum(keep, sends, pieces, count, meanwhile):
    bits = [1 << i for i in range(1, count.bit_length() - 1)]
    held, at = [], 0
    for send, n in zip(sends, pieces):
        got = swap(send, 1, count)
        held.append({p: (keep[p, at:at + n], got[p]) for p in range(count // 2)})
        at += n
    other = meanwhile(got)
    done = []
    for i, (v, n) in enumerate(zip(held, pieces)):
        order = bits if i < (len(pieces) + 1) // 2 else bits[1:] + bits[:1]
        for k in order:
            v = {p: a + b for p, (a, b) in v.items()}
            away = [p for p in sorted(v) if p & (k // 2)]
            got = swap(jnp.concatenate([v[p] for p in away], axis=0), k, count)
            v = {p ^ (k // 2): (v[p ^ (k // 2)], got[j * n:(j + 1) * n]) for j, p in enumerate(away)}
        done += v[0]
    return done, other


def gradient_kernel(pieces, scale, *refs):
    weight_ref, mine_ref = refs[:2]
    terms, (out_ref, col_ref) = refs[2:-2], refs[-2:]
    share, width = mine_ref.shape
    pair = 2 * share
    me = lax.axis_index("cols")
    lo = pl.multiple_of((me // 2) * pair, pair)
    for l in range(pair // LANES):
        at = pl.multiple_of(lo + l * LANES, LANES)
        col_ref[pl.ds(l * LANES, LANES), :] = column(weight_ref[:, pl.ds(at, LANES)])
    at = 0
    for i, n in enumerate(pieces):
        col = col_ref[pl.ds(pl.multiple_of((me % 2) * share + at, 8), n), :]
        for l in range(width // LANES):
            ls = pl.ds(l * LANES, LANES)
            out_ref[pl.ds(at, n), ls] = scale * (
                col * mine_ref[pl.ds(at, n), ls] - (terms[2 * i][:, ls] + terms[2 * i + 1][:, ls])
            )
        at += n


def gradient(pieces, scale, weight, mine, terms):
    share, width = mine.shape
    return pl.pallas_call(
        functools.partial(gradient_kernel, pieces, float(scale)),
        out_shape=jax.ShapeDtypeStruct((share, width), F32),
        in_specs=full(2 + len(terms)),
        out_specs=full(1)[0],
        scratch_shapes=[pltpu.VMEM((2 * share, LANES), F32)],
        compiler_params=params(8),
        name="gradient",
    )(weight, mine, *terms)


def combine(x, count, join):
    k = 1
    while k < count:
        if 4 * k <= count:
            x = join([x] + [swap(x, j * k, count) for j in (1, 2, 3)])
            k *= 4
        else:
            x = join([x, swap(x, k, count)])
            k *= 2
    return x


def add_join(xs):
    return tree(jnp.add, xs)


def lse_join(xs):
    m = tree(jnp.maximum, xs)
    return m + jnp.log2(tree(jnp.add, [jnp.exp2(x - m) for x in xs]))


def local(new_points, arch_points, new_mass, arch_mass):
    rows = new_points.shape[0]
    count = lax.axis_size("cols")
    assert count & (count - 1) == 0
    reduce_add = functools.partial(combine, count=count, join=add_join)
    reduce_lse = functools.partial(combine, count=count, join=lse_join)
    total_cols = arch_points.shape[0] * count
    share = rows // count
    a = (new_mass / rows).reshape(1, rows)

    z, b, sq, lse, mine = scores(new_points, arch_points, arch_mass, total_cols, share)
    alpha = -reduce_lse(lse)
    e, n, r, br, vbr, part = plan(z, b, sq, jnp.log2(a) + alpha)
    u2 = a / reduce_add(part)
    bv2, part = sweep("fwd", e, b, u2)
    u3 = a / reduce_add(part)
    bv3, part = sweep("fwd", e, b, u3)
    fbar3 = a + u3 * reduce_add(part)
    w3 = u3 * fbar3 / a
    mid, part = sweep("mid", e, b, bv2, w3)
    fbar2 = u2 * reduce_add(part)
    w2 = u2 * fbar2 / a
    gb1, part = sweep("bwd", e, br, r, w2)
    fbar1 = reduce_add(part)
    w1 = fbar1 / a
    pieces = [share * f // 16 for f in (6, 6, 4)]
    half, keep, sends = mix(
        share, pieces, e, arch_points, (bv3, bv2, mid, br, vbr, gb1), (u3, w3, u2, w2, w1)
    )
    terms, (pot, arch_grad, new_pot) = scatter_sum(
        keep, sends, pieces, count,
        lambda after: back(
            total_cols, half, new_points, arch_points, e, b, r, n, sq, bv2, bv3, mid, gb1, vbr, w1,
            alpha, u3, after
        ),
    )
    row_weight = 2.0 * (fbar3 + fbar2 + fbar1) - a
    new_grad = gradient(pieces, rows, row_weight, mine, terms)
    return (new_pot.reshape(-1), pot.reshape(-1), new_grad, arch_grad)


def solution(mesh):
    in_specs = (P("pairs", None), P(("pairs", "cols"), None), P("pairs"), P(("pairs", "cols")))
    out_specs = (
        P("pairs"),
        P(("pairs", "cols")),
        P(("pairs", "cols"), None),
        P(("pairs", "cols"), None),
    )
    return jax.shard_map(local, mesh=mesh, in_specs=in_specs, out_specs=out_specs, check_vma=False)
```

```python
import functools
import math
import jax
import jax.numpy as jnp
from jax import lax
from jax.experimental import pallas as pl
from jax.experimental.pallas import tpu as pltpu
from jax.sharding import PartitionSpec as P

EPSILON = 0.05
LOGK = math.log2(math.e) / EPSILON
LANES = 128
SUB = 8
VMEM = pltpu.VMEM
F32 = jnp.float32
BF16 = jnp.bfloat16


def params(mib=28):
    return pltpu.CompilerParams(vmem_limit_bytes=mib * 1024 * 1024)


def full(n):
    return [pl.BlockSpec(memory_space=VMEM)] * n


def column(row):
    return jnp.transpose(jnp.broadcast_to(row, (LANES, LANES)))


def lanes(x):
    return [x[:, l * LANES:(l + 1) * LANES] for l in range(x.shape[1] // LANES)]


def wide(x):
    return jnp.broadcast_to(x, (SUB, LANES))


def tree(op, xs):
    xs = list(xs)
    while len(xs) > 1:
        xs = [op(xs[i], xs[i + 1]) if i + 1 < len(xs) else xs[i] for i in range(0, len(xs), 2)]
    return xs[0]


def lane_sum(xs):
    return wide(jnp.sum(tree(jnp.add, xs), axis=1, keepdims=True))


def lane_max(xs):
    return wide(jnp.max(tree(jnp.maximum, xs), axis=1, keepdims=True))


def rows_of(i, n):
    return pl.ds(pl.multiple_of(i * n, n), n)


def scores_kernel(total_cols, share, x_ref, y_ref, mass_ref, z_ref, b_ref, sq_ref, lse_ref, mine_ref,
                  cb_ref):
    cols, width = y_ref.shape
    rows = x_ref.shape[0]
    first = pl.multiple_of(lax.axis_index("cols") * share, share)
    mine_ref[...] = x_ref[pl.ds(first, share), :].astype(F32)
    for c in range(cols // LANES):
        s = pl.ds(c * LANES, LANES)
        b = column(mass_ref[:, s] * (1.0 / total_cols))
        b_ref[s, :] = b
        yf = y_ref[s, :].astype(F32)
        sq = jnp.sum(yf * yf, axis=1, keepdims=True) * (LOGK / width)
        sq = jnp.broadcast_to(sq, (LANES, LANES))
        sq_ref[s, :] = sq
        cb_ref[s, :] = jnp.log2(b) - sq
    step = 2 * LANES
    many = 4

    def reduce_block(r):
        for l in range(step // LANES):
            ls = pl.ds(r * step + l * LANES, LANES)
            m = [None] * many
            for g in range(cols // SUB):
                s = pl.ds(g * SUB, SUB)
                v = z_ref[s, ls] + cb_ref[s, :]
                m[g % many] = v if m[g % many] is None else jnp.maximum(m[g % many], v)
            m = jnp.max(tree(jnp.maximum, m), axis=0, keepdims=True)
            mw = wide(m)
            t = [None] * many
            for g in range(cols // SUB):
                s = pl.ds(g * SUB, SUB)
                v = jnp.exp2(z_ref[s, ls] + cb_ref[s, :] - mw)
                t[g % many] = v if t[g % many] is None else t[g % many] + v
            lse_ref[:, ls] = m + jnp.log2(jnp.sum(tree(jnp.add, t), axis=0, keepdims=True))

    for r in range(rows // step):
        s = pl.ds(r * step, step)
        z_ref[:, s] = lax.dot_general(
            y_ref[...], x_ref[s, :], (((1,), (1,)), ((), ())), preferred_element_type=F32
        ) * (2.0 * LOGK / width)
        if r > 0:
            reduce_block(r - 1)
    reduce_block(rows // step - 1)


def scores(new_points, arch_points, arch_mass, total_cols, share):
    rows, cols = new_points.shape[0], arch_points.shape[0]
    return pl.pallas_call(
        functools.partial(scores_kernel, total_cols, share),
        out_shape=(
            VMEM((cols, rows), F32),
            VMEM((cols, LANES), F32),
            VMEM((cols, LANES), F32),
            jax.ShapeDtypeStruct((1, rows), F32),
            VMEM((share, new_points.shape[1]), F32),
        ),
        in_specs=full(3),
        out_specs=tuple(full(5)),
        scratch_shapes=[pltpu.VMEM((cols, LANES), F32)],
        compiler_params=params(),
        name="scores",
    )(new_points, arch_points, arch_mass.reshape(1, cols))


CHUNK = 128


def groups(i):
    return [pl.ds(pl.multiple_of(i * CHUNK, CHUNK) + h * SUB, SUB) for h in range(CHUNK // SUB)]


def column_dots(e_ref, w, tmp_ref):
    def body(i, carry):
        for s in groups(i):
            tmp_ref[s, :] = tree(jnp.add, [a * c for a, c in zip(lanes(e_ref[s, :]), w)])
        return carry

    lax.fori_loop(0, e_ref.shape[0] // CHUNK, body, 0)


def row_sums(e_ref, c_ref, part_ref):
    def body(i, acc):
        for s in groups(i):
            c = c_ref[s, :]
            acc = [a + d * c for a, d in zip(acc, lanes(e_ref[s, :]))]
        return acc

    cols, rows = e_ref.shape
    acc = lax.fori_loop(0, cols // CHUNK, body, [jnp.zeros((SUB, LANES), F32)] * (rows // LANES))
    for l, a in enumerate(acc):
        part_ref[:, pl.ds(l * LANES, LANES)] = jnp.sum(a, axis=0, keepdims=True)


def spread(x, op):
    return jnp.broadcast_to(op(x, axis=1, keepdims=True), x.shape)


def plan_kernel(z_ref, b_ref, sq_ref, w_ref, e_ref, n_ref, r_ref, br_ref, vbr_ref, part_ref, tmp_ref):
    cols, rows = z_ref.shape
    w = [wide(a) for a in lanes(w_ref[...])]

    def top(i, carry):
        for s in groups(i):
            tmp_ref[s, :] = tree(jnp.maximum, [a + c for a, c in zip(lanes(z_ref[s, :]), w)])
        return carry

    lax.fori_loop(0, cols // CHUNK, top, 0)

    def spread_top(i, carry):
        s = rows_of(i, CHUNK)
        n_ref[s, :] = spread(tmp_ref[s, :], jnp.max)
        return carry

    lax.fori_loop(0, cols // CHUNK, spread_top, 0)

    def powers(i, carry):
        for s in groups(i):
            n = n_ref[s, :]
            e = [jnp.exp2(a + c - n) for a, c in zip(lanes(z_ref[s, :]), w)]
            for l, a in enumerate(e):
                e_ref[s, pl.ds(l * LANES, LANES)] = a
            tmp_ref[s, :] = tree(jnp.add, e)
        return carry

    lax.fori_loop(0, cols // CHUNK, powers, 0)

    def scale(i, carry):
        s = rows_of(i, CHUNK)
        t = spread(tmp_ref[s, :], jnp.sum)
        r = 1.0 / t
        br = b_ref[s, :] * r
        r_ref[s, :] = r
        br_ref[s, :] = br
        vbr_ref[s, :] = br * jnp.exp2(n_ref[s, :] + jnp.log2(t) - sq_ref[s, :])
        return carry

    lax.fori_loop(0, cols // CHUNK, scale, 0)
    row_sums(e_ref, br_ref, part_ref)


def plan(z, b, sq, w):
    cols, rows = z.shape
    return pl.pallas_call(
        plan_kernel,
        out_shape=(VMEM((cols, rows), F32),) + (VMEM((cols, LANES), F32),) * 4
        + (jax.ShapeDtypeStruct((1, rows), F32),),
        in_specs=full(4),
        out_specs=tuple(full(6)),
        scratch_shapes=[pltpu.VMEM((cols, LANES), F32)],
        input_output_aliases={0: 0},
        compiler_params=params(8),
        name="plan",
    )(z, b, sq, w)


def sweep_kernel(kind, e_ref, b_ref, *refs):
    cols, rows = e_ref.shape
    more = refs[:-4]
    w_ref, c_ref, part_ref, tmp_ref = refs[-4:]
    column_dots(e_ref, [wide(a) for a in lanes(w_ref[...])], tmp_ref)

    def weigh(i, carry):
        s = rows_of(i, CHUNK)
        t = spread(tmp_ref[s, :], jnp.sum)
        b = b_ref[s, :]
        if kind == "fwd":
            c = b / t
        elif kind == "mid":
            v = more[0][s, :]
            c = v * v * t / b
        else:
            c = b * t * more[0][s, :]
        c_ref[s, :] = c
        return carry

    lax.fori_loop(0, cols // CHUNK, weigh, 0)
    row_sums(e_ref, c_ref, part_ref)


def sweep(kind, e, b, *more):
    cols, rows = e.shape
    return pl.pallas_call(
        functools.partial(sweep_kernel, kind),
        out_shape=(VMEM((cols, LANES), F32), jax.ShapeDtypeStruct((1, rows), F32)),
        in_specs=full(2 + len(more)),
        out_specs=tuple(full(2)),
        scratch_shapes=[pltpu.VMEM((cols, LANES), F32)],
        compiler_params=params(8),
        name="sweep_" + kind,
    )(e, b, *more)


def mix_kernel(share, pieces, e_ref, y_ref, *refs):
    c_refs, r_refs = refs[:6], refs[6:11]
    half_ref, prod_ref = refs[11], refs[-1]
    keep_refs, send_refs = refs[12:-1:2], refs[13:-1:2]
    cols, rows = e_ref.shape
    pair = 2 * share
    me = lax.axis_index("cols")
    core = me % 2
    for p in range(rows // pair):
        lo = pl.multiple_of(((me // 2) ^ p) * pair, pair)
        spots = [pl.ds(pl.multiple_of(lo + l * LANES, LANES), LANES) for l in range(pair // LANES)]
        r = [[wide(ref[:, ls]) for ref in r_refs] for ls in spots]
        for g in range(cols // (2 * SUB)):
            outs = [[] for _ in spots]
            for h in range(2):
                s = pl.ds(g * 2 * SUB + h * SUB, SUB)
                c = [ref[s, :] for ref in c_refs]
                for o, rl, ls in zip(outs, r, spots):
                    terms = [a * b for a, b in zip(c, rl)] + [c[5]]
                    o.append(e_ref[s, ls] * tree(jnp.add, terms))
            for o, ls in zip(outs, spots):
                half_ref[pl.ds(g * 2 * SUB, 2 * SUB), ls] = jnp.concatenate(o, axis=0).astype(BF16)
        prod_ref[p % 2] = lax.dot_general(
            half_ref[:, pl.ds(lo, pair)], y_ref[...], (((0,), (0,)), ((), ())),
            preferred_element_type=F32,
        )
        for refs, side in ((keep_refs, core), (send_refs, 1 - core)):
            at = side * share
            for ref, (n, bits) in zip(refs, pieces):
                ref[spot(p, bits)] = prod_ref[p % 2, pl.ds(pl.multiple_of(at, SUB), n), :]
                at = at + n


def spot(p, bits):
    return sum(bool(2 * p & k) << i for i, k in enumerate(reversed(bits)))


def mix(share, pieces, e, y, columns, weights):
    cols, rows = e.shape
    width = y.shape[1]
    out = [VMEM((cols, rows), BF16)]
    for n, _ in pieces:
        out += [jax.ShapeDtypeStruct((rows // (2 * share), n, width), F32)] * 2
    half, *got = pl.pallas_call(
        functools.partial(mix_kernel, share, pieces),
        out_shape=tuple(out),
        in_specs=full(13),
        out_specs=tuple(full(len(out))),
        scratch_shapes=[pltpu.VMEM((2, 2 * share, width), F32)],
        compiler_params=params(16),
        name="mix",
    )(e, y, *columns, *weights)
    return half, got[0::2], got[1::2]


def back_kernel(total_cols, half_ref, x_ref, y_ref, e_ref, b_ref, r_ref, n_ref, sq_ref, bv2_ref,
                bv3_ref, mid_ref, gb1_ref, vbr_ref, w_ref, alpha_ref, u3_ref, after_ref, pot_ref, arch_ref,
                new_ref, tmp_ref):
    del after_ref
    cols, rows = e_ref.shape
    width = y_ref.shape[1]
    column_dots(e_ref, [wide(a) for a in lanes(w_ref[...])], tmp_ref)
    step = 256
    for j in range(cols // step):
        s = pl.ds(j * step, step)
        b = b_ref[s, :]
        gb0 = vbr_ref[s, :] * spread(tmp_ref[s, :], jnp.sum)
        gb2 = mid_ref[s, :] * b / bv2_ref[s, :]
        tr = b + 2.0 * (gb2 + gb1_ref[s, :] / r_ref[s, :]) + gb0
        back = jnp.dot(half_ref[s, :], x_ref[...], preferred_element_type=F32)
        for l in range(width // LANES):
            ls = slice(l * LANES, (l + 1) * LANES)
            arch_ref[s, ls] = total_cols * (tr * y_ref[s, ls].astype(F32) - back[:, ls])
    for c in range(cols // LANES):
        s = pl.ds(c * LANES, LANES)
        pot = (sq_ref[s, :] - n_ref[s, :] + jnp.log2(bv3_ref[s, :] / b_ref[s, :])) * (1.0 / LOGK)
        pot_ref[:, s] = jnp.transpose(pot)[0:1, :]
    ones = jnp.ones((SUB, width), BF16)
    for i in range(rows // step):
        s = pl.ds(i * step, step)
        xf = x_ref[s, :].astype(F32)
        square = xf * xf
        high = square.astype(BF16)
        low = (square - high.astype(F32)).astype(BF16)
        sq = sum(
            lax.dot_general(ones, v, (((1,), (1,)), ((), ())), preferred_element_type=F32)
            for v in (high, low)
        )[0:1, :] * (LOGK / width)
        new_ref[:, s] = (alpha_ref[:, s] + jnp.log2(u3_ref[:, s]) + sq) * (1.0 / LOGK)


def back(total_cols, half, x, y, *rest):
    cols, rows = half.shape
    width = y.shape[1]
    return pl.pallas_call(
        functools.partial(back_kernel, float(total_cols)),
        out_shape=(
            jax.ShapeDtypeStruct((1, cols), F32),
            jax.ShapeDtypeStruct((cols, width), F32),
            jax.ShapeDtypeStruct((1, rows), F32),
        ),
        in_specs=full(2 + len(rest)) + [pl.BlockSpec(memory_space=pl.ANY)],
        out_specs=tuple(full(3)),
        scratch_shapes=[pltpu.VMEM((cols, LANES), F32)],
        compiler_params=params(16),
        cost_estimate=pl.CostEstimate(
            flops=2 * cols * rows * width, bytes_accessed=16 * 1024 * 1024, transcendentals=0
        ),
        name="back",
    )(half, x, y, *rest)


def swap(v, k, count):
    return lax.ppermute(v, "cols", [(i, i ^ k) for i in range(count)])


def fold_kernel(keep_ref, got_ref, after_ref, stay_ref, away_ref):
    del after_ref
    half = keep_ref.shape[0] // 2
    for i in range(half):
        stay_ref[i] = keep_ref[i] + got_ref[i]
        away_ref[i] = keep_ref[half + i] + got_ref[half + i]


def fold(keep, got, after):
    blocks, n, width = keep.shape
    return pl.pallas_call(
        fold_kernel,
        out_shape=(jax.ShapeDtypeStruct((blocks // 2, n, width), F32),) * 2,
        in_specs=full(2) + [pl.BlockSpec(memory_space=pl.ANY)],
        out_specs=tuple(full(2)),
        compiler_params=params(8),
        name="fold",
    )(keep, got, after)


def scatter_sum(keeps, sends, pieces, count, after, meanwhile):
    keeps = list(keeps)
    gots = [swap(send, 1, count) for send in sends]

    def advance(i, step, after):
        keeps[i], away = fold(keeps[i], gots[i], after)
        gots[i] = swap(away, pieces[i][1][step], count)
        return away

    steps = count.bit_length() - 2
    other = None
    for t in range(steps + 1):
        turn = [(0, t), (1, t), (2, t)] if t == 0 else [(2, t), (0, t)] + [(1, t - 1)] * (t > 1)
        for i, step in turn:
            if step < steps:
                after = advance(i, step, after)
        if t == 0:
            other = meanwhile(after)
            after = other[0]
    return [x[0] for pair in zip(keeps, gots) for x in pair], other


def gradient_kernel(pieces, scale, *refs):
    weight_ref, mine_ref = refs[:2]
    terms, (out_ref, col_ref) = refs[2:-2], refs[-2:]
    share, width = mine_ref.shape
    pair = 2 * share
    me = lax.axis_index("cols")
    lo = pl.multiple_of((me // 2) * pair, pair)
    for l in range(pair // LANES):
        at = pl.multiple_of(lo + l * LANES, LANES)
        col_ref[pl.ds(l * LANES, LANES), :] = column(weight_ref[:, pl.ds(at, LANES)])
    at = 0
    for i, (n, _) in enumerate(pieces):
        col = col_ref[pl.ds(pl.multiple_of((me % 2) * share + at, 8), n), :]
        for l in range(width // LANES):
            ls = pl.ds(l * LANES, LANES)
            out_ref[pl.ds(at, n), ls] = scale * (
                col * mine_ref[pl.ds(at, n), ls] - (terms[2 * i][:, ls] + terms[2 * i + 1][:, ls])
            )
        at += n


def gradient(pieces, scale, weight, mine, terms):
    share, width = mine.shape
    return pl.pallas_call(
        functools.partial(gradient_kernel, pieces, float(scale)),
        out_shape=jax.ShapeDtypeStruct((share, width), F32),
        in_specs=full(2 + len(terms)),
        out_specs=full(1)[0],
        scratch_shapes=[pltpu.VMEM((2 * share, LANES), F32)],
        compiler_params=params(8),
        name="gradient",
    )(weight, mine, *terms)


def combine(x, count, join):
    k = 1
    while k < count:
        if 4 * k <= count:
            x = join([x] + [swap(x, j * k, count) for j in (1, 2, 3)])
            k *= 4
        else:
            x = join([x, swap(x, k, count)])
            k *= 2
    return x


def add_join(xs):
    return tree(jnp.add, xs)


def lse_join(xs):
    m = tree(jnp.maximum, xs)
    return m + jnp.log2(tree(jnp.add, [jnp.exp2(x - m) for x in xs]))


def routes(share, count):
    bits = [1 << i for i in range(1, count.bit_length() - 1)]
    units = share // SUB
    first = units * 6 // 16
    last = units - 2 * first
    return [(first * SUB, bits), (first * SUB, bits), (last * SUB, bits[1:] + bits[:1])]


def local(new_points, arch_points, new_mass, arch_mass):
    rows = new_points.shape[0]
    count = lax.axis_size("cols")
    assert count & (count - 1) == 0
    reduce_add = functools.partial(combine, count=count, join=add_join)
    reduce_lse = functools.partial(combine, count=count, join=lse_join)
    total_cols = arch_points.shape[0] * count
    share = rows // count
    a = (new_mass / rows).reshape(1, rows)

    z, b, sq, lse, mine = scores(new_points, arch_points, arch_mass, total_cols, share)
    alpha = -reduce_lse(lse)
    e, n, r, br, vbr, part = plan(z, b, sq, jnp.log2(a) + alpha)
    u2 = a / reduce_add(part)
    bv2, part = sweep("fwd", e, b, u2)
    u3 = a / reduce_add(part)
    bv3, part = sweep("fwd", e, b, u3)
    fbar3 = a + u3 * reduce_add(part)
    w3 = u3 * fbar3 / a
    mid, part = sweep("mid", e, b, bv2, w3)
    fbar2 = u2 * reduce_add(part)
    w2 = u2 * fbar2 / a
    gb1, part = sweep("bwd", e, br, r, w2)
    fbar1 = reduce_add(part)
    w1 = fbar1 / a
    pieces = routes(share, count)
    half, keeps, sends = mix(
        share, pieces, e, arch_points, (bv3, bv2, mid, br, vbr, gb1), (u3, w3, u2, w2, w1)
    )
    terms, (pot, arch_grad, new_pot) = scatter_sum(
        keeps, sends, pieces, count, part,
        lambda after: back(
            total_cols, half, new_points, arch_points, e, b, r, n, sq, bv2, bv3, mid, gb1, vbr, w1,
            alpha, u3, after
        ),
    )
    row_weight = 2.0 * (fbar3 + fbar2 + fbar1) - a
    new_grad = gradient(pieces, rows, row_weight, mine, terms)
    return (new_pot.reshape(-1), pot.reshape(-1), new_grad, arch_grad)


def solution(mesh):
    in_specs = (P("pairs", None), P(("pairs", "cols"), None), P("pairs"), P(("pairs", "cols")))
    out_specs = (
        P("pairs"),
        P(("pairs", "cols")),
        P(("pairs", "cols"), None),
        P(("pairs", "cols"), None),
    )
    return jax.shard_map(local, mesh=mesh, in_specs=in_specs, out_specs=out_specs, check_vma=False)
```

```python
import functools
import math
import jax
import jax.numpy as jnp
from jax import lax
from jax.experimental import pallas as pl
from jax.experimental.pallas import tpu as pltpu
from jax.sharding import PartitionSpec as P

EPSILON = 0.05
LOGK = math.log2(math.e) / EPSILON
LANES = 128
SUB = 8
VMEM = pltpu.VMEM
F32 = jnp.float32
BF16 = jnp.bfloat16


def params(mib=28):
    return pltpu.CompilerParams(vmem_limit_bytes=mib * 1024 * 1024)


def full(n):
    return [pl.BlockSpec(memory_space=VMEM)] * n


def column(row):
    return jnp.transpose(jnp.broadcast_to(row, (LANES, LANES)))


def lanes(x):
    return [x[:, l * LANES:(l + 1) * LANES] for l in range(x.shape[1] // LANES)]


def wide(x):
    return jnp.broadcast_to(x, (SUB, LANES))


def tree(op, xs):
    xs = list(xs)
    while len(xs) > 1:
        xs = [op(xs[i], xs[i + 1]) if i + 1 < len(xs) else xs[i] for i in range(0, len(xs), 2)]
    return xs[0]


def lane_sum(xs):
    return wide(jnp.sum(tree(jnp.add, xs), axis=1, keepdims=True))


def lane_max(xs):
    return wide(jnp.max(tree(jnp.maximum, xs), axis=1, keepdims=True))


def rows_of(i, n):
    return pl.ds(pl.multiple_of(i * n, n), n)


def scores_kernel(total_cols, share, x_hbm, y_hbm, mass_hbm, z_ref, b_ref, sq_ref, lse_ref, mine_ref,
                  cb_ref, x_ref, y_ref, mass_ref, sems):
    cols, width = y_ref.shape
    rows = x_ref.shape[0]
    step = 2 * LANES
    copies = [
        pltpu.make_async_copy(hbm, ref, sems.at[i])
        for i, (hbm, ref) in enumerate(((x_hbm, x_ref), (y_hbm, y_ref), (mass_hbm, mass_ref)))
    ]
    for copy in copies:
        copy.start()
    for copy in copies:
        copy.wait()
    for c in range(cols // LANES):
        s = pl.ds(c * LANES, LANES)
        b = column(mass_ref[:, s] * (1.0 / total_cols))
        b_ref[s, :] = b
        yf = y_ref[s, :].astype(F32)
        sq = jnp.sum(yf * yf, axis=1, keepdims=True) * (LOGK / width)
        sq = jnp.broadcast_to(sq, (LANES, LANES))
        sq_ref[s, :] = sq
        cb_ref[s, :] = jnp.log2(b) - sq
    many = 4

    def reduce_block(r):
        for l in range(step // LANES):
            ls = pl.ds(r * step + l * LANES, LANES)
            m = [None] * many
            for g in range(cols // SUB):
                s = pl.ds(g * SUB, SUB)
                v = z_ref[s, ls] + cb_ref[s, :]
                m[g % many] = v if m[g % many] is None else jnp.maximum(m[g % many], v)
            m = jnp.max(tree(jnp.maximum, m), axis=0, keepdims=True)
            mw = wide(m)
            t = [None] * many
            for g in range(cols // SUB):
                s = pl.ds(g * SUB, SUB)
                v = jnp.exp2(z_ref[s, ls] + cb_ref[s, :] - mw)
                t[g % many] = v if t[g % many] is None else t[g % many] + v
            lse_ref[:, ls] = m + jnp.log2(jnp.sum(tree(jnp.add, t), axis=0, keepdims=True))

    for r in range(rows // step):
        s = pl.ds(r * step, step)
        z_ref[:, s] = lax.dot_general(
            y_ref[...], x_ref[s, :], (((1,), (1,)), ((), ())), preferred_element_type=F32
        ) * (2.0 * LOGK / width)
        if r > 0:
            reduce_block(r - 1)
    reduce_block(rows // step - 1)
    first = pl.multiple_of(lax.axis_index("cols") * share, share)
    mine_ref[...] = x_ref[pl.ds(first, share), :].astype(F32)


def scores(new_points, arch_points, arch_mass, total_cols, share):
    rows, cols = new_points.shape[0], arch_points.shape[0]
    return pl.pallas_call(
        functools.partial(scores_kernel, total_cols, share),
        out_shape=(
            VMEM((cols, rows), F32),
            VMEM((cols, LANES), F32),
            VMEM((cols, LANES), F32),
            jax.ShapeDtypeStruct((1, rows), F32),
            VMEM((share, new_points.shape[1]), F32),
        ),
        in_specs=[pl.BlockSpec(memory_space=pltpu.HBM)] * 3,
        out_specs=tuple(full(5)),
        scratch_shapes=[
            pltpu.VMEM((cols, LANES), F32),
            pltpu.VMEM(new_points.shape, BF16),
            pltpu.VMEM(arch_points.shape, BF16),
            pltpu.VMEM((1, cols), F32),
            pltpu.SemaphoreType.DMA((3,)),
        ],
        compiler_params=params(50),
        name="scores",
    )(new_points, arch_points, arch_mass.reshape(1, cols))


CHUNK = 512


def groups(i):
    return [pl.ds(pl.multiple_of(i * CHUNK, CHUNK) + h * SUB, SUB) for h in range(CHUNK // SUB)]


def column_dots(e_ref, w, tmp_ref):
    def body(i, carry):
        for s in groups(i):
            tmp_ref[s, :] = tree(jnp.add, [a * c for a, c in zip(lanes(e_ref[s, :]), w)])
        return carry

    lax.fori_loop(0, e_ref.shape[0] // CHUNK, body, 0)


def row_sums(e_ref, c_ref, part_ref):
    def body(i, acc):
        for s in groups(i):
            c = c_ref[s, :]
            acc = [a + d * c for a, d in zip(acc, lanes(e_ref[s, :]))]
        return acc

    cols, rows = e_ref.shape
    acc = lax.fori_loop(0, cols // CHUNK, body, [jnp.zeros((SUB, LANES), F32)] * (rows // LANES))
    for l, a in enumerate(acc):
        part_ref[:, pl.ds(l * LANES, LANES)] = jnp.sum(a, axis=0, keepdims=True)


def spread(x, op):
    return jnp.broadcast_to(op(x, axis=1, keepdims=True), x.shape)


def plan_kernel(z_ref, b_ref, sq_ref, w_ref, e_ref, n_ref, r_ref, br_ref, vbr_ref, part_ref, tmp_ref):
    cols, rows = z_ref.shape
    w = [wide(a) for a in lanes(w_ref[...])]

    def top(i, carry):
        for s in groups(i):
            tmp_ref[s, :] = tree(jnp.maximum, [a + c for a, c in zip(lanes(z_ref[s, :]), w)])
        return carry

    lax.fori_loop(0, cols // CHUNK, top, 0)

    def spread_top(i, carry):
        s = rows_of(i, CHUNK)
        n_ref[s, :] = spread(tmp_ref[s, :], jnp.max)
        return carry

    lax.fori_loop(0, cols // CHUNK, spread_top, 0)

    def powers(i, carry):
        for s in groups(i):
            n = n_ref[s, :]
            e = [jnp.exp2(a + c - n) for a, c in zip(lanes(z_ref[s, :]), w)]
            for l, a in enumerate(e):
                e_ref[s, pl.ds(l * LANES, LANES)] = a
            tmp_ref[s, :] = tree(jnp.add, e)
        return carry

    lax.fori_loop(0, cols // CHUNK, powers, 0)

    def scale(i, carry):
        s = rows_of(i, CHUNK)
        t = spread(tmp_ref[s, :], jnp.sum)
        r = 1.0 / t
        br = b_ref[s, :] * r
        r_ref[s, :] = r
        br_ref[s, :] = br
        vbr_ref[s, :] = br * jnp.exp2(n_ref[s, :] + jnp.log2(t) - sq_ref[s, :])
        return carry

    lax.fori_loop(0, cols // CHUNK, scale, 0)
    row_sums(e_ref, br_ref, part_ref)


def plan(z, b, sq, w):
    cols, rows = z.shape
    return pl.pallas_call(
        plan_kernel,
        out_shape=(VMEM((cols, rows), F32),) + (VMEM((cols, LANES), F32),) * 4
        + (jax.ShapeDtypeStruct((1, rows), F32),),
        in_specs=full(4),
        out_specs=tuple(full(6)),
        scratch_shapes=[pltpu.VMEM((cols, LANES), F32)],
        input_output_aliases={0: 0},
        compiler_params=params(8),
        name="plan",
    )(z, b, sq, w)


def sweep_kernel(kind, e_ref, b_ref, *refs):
    cols, rows = e_ref.shape
    more = refs[:-4]
    w_ref, c_ref, part_ref, tmp_ref = refs[-4:]
    column_dots(e_ref, [wide(a) for a in lanes(w_ref[...])], tmp_ref)

    def weigh(i, carry):
        s = rows_of(i, CHUNK)
        t = spread(tmp_ref[s, :], jnp.sum)
        b = b_ref[s, :]
        if kind == "fwd":
            c = b / t
        elif kind == "mid":
            v = more[0][s, :]
            c = v * v * t / b
        else:
            c = b * t * more[0][s, :]
        c_ref[s, :] = c
        return carry

    lax.fori_loop(0, cols // CHUNK, weigh, 0)
    row_sums(e_ref, c_ref, part_ref)


def sweep(kind, e, b, *more):
    cols, rows = e.shape
    return pl.pallas_call(
        functools.partial(sweep_kernel, kind),
        out_shape=(VMEM((cols, LANES), F32), jax.ShapeDtypeStruct((1, rows), F32)),
        in_specs=full(2 + len(more)),
        out_specs=tuple(full(2)),
        scratch_shapes=[pltpu.VMEM((cols, LANES), F32)],
        compiler_params=params(8),
        name="sweep_" + kind,
    )(e, b, *more)


def mix_kernel(share, pieces, e_ref, y_ref, *refs):
    c_refs, r_refs = refs[:6], refs[6:11]
    half_ref, (prod_ref, left_ref, right_ref) = refs[11], refs[-3:]
    keep_refs, send_refs = refs[12:-3:2], refs[13:-3:2]
    cols, rows = e_ref.shape
    pair = 2 * share
    me = lax.axis_index("cols")
    core = me % 2
    entry = lax.broadcasted_iota(jnp.int32, (SUB, LANES), 1)
    for g in range(cols // (2 * SUB)):
        outs = []
        for h in range(2):
            s = pl.ds(g * 2 * SUB + h * SUB, SUB)
            outs.append(split_parts([ref[s, :] for ref in c_refs], entry, LEFT))
        left_ref[pl.ds(g * 2 * SUB, 2 * SUB), :] = jnp.concatenate(outs, axis=0).astype(BF16)
    for l in range(rows // LANES):
        ls = pl.ds(l * LANES, LANES)
        r = [wide(ref[:, ls]) for ref in r_refs] + [jnp.ones((SUB, LANES), F32)]
        for g in range(LANES // (2 * SUB)):
            outs = []
            for h in range(2):
                at = lax.broadcasted_iota(jnp.int32, (SUB, LANES), 0) + (2 * g + h) * SUB
                outs.append(split_parts(r, at, RIGHT) if (2 * g + h) * SUB < 36 else jnp.zeros((SUB, LANES), F32))
            right_ref[pl.ds(g * 2 * SUB, 2 * SUB), ls] = jnp.concatenate(outs, axis=0).astype(BF16)
    for p in range(rows // pair):
        lo = pl.multiple_of(((me // 2) ^ p) * pair, pair)
        block = pl.ds(lo, pair)
        for g in range(cols // MIX):
            s = pl.ds(g * MIX, MIX)
            scale = jnp.dot(left_ref[s, :], right_ref[:, block], preferred_element_type=F32)
            half_ref[s, block] = (e_ref[s, block] * scale).astype(BF16)
        prod_ref[p % 2] = lax.dot_general(
            half_ref[:, block], y_ref[...], (((0,), (0,)), ((), ())),
            preferred_element_type=F32,
        )
        for refs, side in ((keep_refs, core), (send_refs, 1 - core)):
            at = side * share
            for ref, (n, bits) in zip(refs, pieces):
                ref[spot(p, bits)] = prod_ref[p % 2, pl.ds(pl.multiple_of(at, SUB), n), :]
                at = at + n


LEFT = (0, 0, 1, 0, 1, 2)
RIGHT = (0, 1, 0, 2, 1, 0)
MIX = 256


def split_parts(values, entry, which):
    x = jnp.zeros_like(values[0])
    for t, v in enumerate(values):
        x = jnp.where((entry >= 6 * t) & (entry < 6 * t + 6), v, x)
    first = x.astype(BF16).astype(F32)
    rest = x - first
    second = rest.astype(BF16).astype(F32)
    part = sum(jnp.where(entry % 6 == q, w, 0) for q, w in enumerate(which))
    return jnp.where(part == 0, first, jnp.where(part == 1, second, rest - second))


def spot(p, bits):
    return sum(bool(2 * p & k) << i for i, k in enumerate(reversed(bits)))


def mix(share, pieces, e, y, columns, weights):
    cols, rows = e.shape
    width = y.shape[1]
    out = [VMEM((cols, rows), BF16)]
    for n, _ in pieces:
        out += [jax.ShapeDtypeStruct((rows // (2 * share), n, width), F32)] * 2
    half, *got = pl.pallas_call(
        functools.partial(mix_kernel, share, pieces),
        out_shape=tuple(out),
        in_specs=full(13),
        out_specs=tuple(full(len(out))),
        scratch_shapes=[
            pltpu.VMEM((2, 2 * share, width), F32),
            pltpu.VMEM((cols, LANES), BF16),
            pltpu.VMEM((LANES, rows), BF16),
        ],
        compiler_params=params(16),
        name="mix",
    )(e, y, *columns, *weights)
    return half, got[0::2], got[1::2]


def back_kernel(total_cols, half_ref, x_ref, y_ref, e_ref, b_ref, r_ref, n_ref, sq_ref, bv2_ref,
                bv3_ref, mid_ref, gb1_ref, vbr_ref, w_ref, alpha_ref, u3_ref, after_ref, pot_ref, arch_ref,
                new_ref, tmp_ref):
    del after_ref
    cols, rows = e_ref.shape
    width = y_ref.shape[1]
    column_dots(e_ref, [wide(a) for a in lanes(w_ref[...])], tmp_ref)
    step = 256
    for j in range(cols // step):
        s = pl.ds(j * step, step)
        b = b_ref[s, :]
        gb0 = vbr_ref[s, :] * spread(tmp_ref[s, :], jnp.sum)
        gb2 = mid_ref[s, :] * b / bv2_ref[s, :]
        tr = b + 2.0 * (gb2 + gb1_ref[s, :] / r_ref[s, :]) + gb0
        back = jnp.dot(half_ref[s, :], x_ref[...], preferred_element_type=F32)
        for l in range(width // LANES):
            ls = slice(l * LANES, (l + 1) * LANES)
            arch_ref[s, ls] = total_cols * (tr * y_ref[s, ls].astype(F32) - back[:, ls])
    for c in range(cols // LANES):
        s = pl.ds(c * LANES, LANES)
        pot = (sq_ref[s, :] - n_ref[s, :] + jnp.log2(bv3_ref[s, :] / b_ref[s, :])) * (1.0 / LOGK)
        pot_ref[:, s] = jnp.transpose(pot)[0:1, :]
    ones = jnp.ones((SUB, width), BF16)
    for i in range(rows // step):
        s = pl.ds(i * step, step)
        xf = x_ref[s, :].astype(F32)
        square = xf * xf
        high = square.astype(BF16)
        low = (square - high.astype(F32)).astype(BF16)
        sq = sum(
            lax.dot_general(ones, v, (((1,), (1,)), ((), ())), preferred_element_type=F32)
            for v in (high, low)
        )[0:1, :] * (LOGK / width)
        new_ref[:, s] = (alpha_ref[:, s] + jnp.log2(u3_ref[:, s]) + sq) * (1.0 / LOGK)


def back(total_cols, half, x, y, *rest):
    cols, rows = half.shape
    width = y.shape[1]
    return pl.pallas_call(
        functools.partial(back_kernel, float(total_cols)),
        out_shape=(
            jax.ShapeDtypeStruct((1, cols), F32),
            jax.ShapeDtypeStruct((cols, width), F32),
            jax.ShapeDtypeStruct((1, rows), F32),
        ),
        in_specs=full(2 + len(rest)) + [pl.BlockSpec(memory_space=pl.ANY)],
        out_specs=tuple(full(3)),
        scratch_shapes=[pltpu.VMEM((cols, LANES), F32)],
        compiler_params=params(16),
        cost_estimate=pl.CostEstimate(
            flops=2 * cols * rows * width, bytes_accessed=16 * 1024 * 1024, transcendentals=0
        ),
        name="back",
    )(half, x, y, *rest)


def swap(v, k, count):
    return lax.ppermute(v, "cols", [(i, i ^ k) for i in range(count)])


def fold_kernel(keep_ref, got_ref, after_ref, stay_ref, away_ref):
    del after_ref
    half = keep_ref.shape[0] // 2
    for i in range(half):
        stay_ref[i] = keep_ref[i] + got_ref[i]
        away_ref[i] = keep_ref[half + i] + got_ref[half + i]


def fold(keep, got, after):
    blocks, n, width = keep.shape
    return pl.pallas_call(
        fold_kernel,
        out_shape=(jax.ShapeDtypeStruct((blocks // 2, n, width), F32),) * 2,
        in_specs=full(2) + [pl.BlockSpec(memory_space=pl.ANY)],
        out_specs=tuple(full(2)),
        compiler_params=params(8),
        name="fold",
    )(keep, got, after)


def scatter_sum(keeps, sends, pieces, count, after, meanwhile):
    keeps = list(keeps)
    gots = [swap(send, 1, count) for send in sends]

    def advance(i, step, after):
        keeps[i], away = fold(keeps[i], gots[i], after)
        gots[i] = swap(away, pieces[i][1][step], count)
        return away

    steps = count.bit_length() - 2
    other = None
    for t in range(steps + 1):
        turn = [(0, t), (1, t), (2, t)] if t == 0 else [(2, t), (0, t)] + [(1, t - 1)] * (t > 1)
        for i, step in turn:
            if step < steps:
                after = advance(i, step, after)
        if t == 0:
            other = meanwhile(after)
            after = other[0]
    return [x[0] for pair in zip(keeps, gots) for x in pair], other


def gradient_kernel(pieces, scale, *refs):
    weight_ref, mine_ref = refs[:2]
    terms, (out_ref, col_ref) = refs[2:-2], refs[-2:]
    share, width = mine_ref.shape
    pair = 2 * share
    me = lax.axis_index("cols")
    lo = pl.multiple_of((me // 2) * pair, pair)
    for l in range(pair // LANES):
        at = pl.multiple_of(lo + l * LANES, LANES)
        col_ref[pl.ds(l * LANES, LANES), :] = column(weight_ref[:, pl.ds(at, LANES)])
    at = 0
    for i, (n, _) in enumerate(pieces):
        col = col_ref[pl.ds(pl.multiple_of((me % 2) * share + at, 8), n), :]
        for l in range(width // LANES):
            ls = pl.ds(l * LANES, LANES)
            out_ref[pl.ds(at, n), ls] = scale * (
                col * mine_ref[pl.ds(at, n), ls] - (terms[2 * i][:, ls] + terms[2 * i + 1][:, ls])
            )
        at += n


def gradient(pieces, scale, weight, mine, terms):
    share, width = mine.shape
    return pl.pallas_call(
        functools.partial(gradient_kernel, pieces, float(scale)),
        out_shape=jax.ShapeDtypeStruct((share, width), F32),
        in_specs=full(2 + len(terms)),
        out_specs=full(1)[0],
        scratch_shapes=[pltpu.VMEM((2 * share, LANES), F32)],
        compiler_params=params(8),
        name="gradient",
    )(weight, mine, *terms)


def combine(x, count, join):
    k = 1
    while k < count:
        if 4 * k <= count:
            x = join([x] + [swap(x, j * k, count) for j in (1, 2, 3)])
            k *= 4
        else:
            x = join([x, swap(x, k, count)])
            k *= 2
    return x


def add_join(xs):
    return tree(jnp.add, xs)


def lse_join(xs):
    m = tree(jnp.maximum, xs)
    return m + jnp.log2(tree(jnp.add, [jnp.exp2(x - m) for x in xs]))


def routes(share, count):
    bits = [1 << i for i in range(1, count.bit_length() - 1)]
    units = share // SUB
    first = units * 6 // 16
    last = units - 2 * first
    return [(first * SUB, bits), (first * SUB, bits), (last * SUB, bits[1:] + bits[:1])]


def local(new_points, arch_points, new_mass, arch_mass):
    rows = new_points.shape[0]
    count = lax.axis_size("cols")
    assert count & (count - 1) == 0
    reduce_add = functools.partial(combine, count=count, join=add_join)
    reduce_lse = functools.partial(combine, count=count, join=lse_join)
    total_cols = arch_points.shape[0] * count
    share = rows // count
    a = (new_mass / rows).reshape(1, rows)

    z, b, sq, lse, mine = scores(new_points, arch_points, arch_mass, total_cols, share)
    alpha = -reduce_lse(lse)
    e, n, r, br, vbr, part = plan(z, b, sq, jnp.log2(a) + alpha)
    u2 = a / reduce_add(part)
    bv2, part = sweep("fwd", e, b, u2)
    u3 = a / reduce_add(part)
    bv3, part = sweep("fwd", e, b, u3)
    fbar3 = a + u3 * reduce_add(part)
    w3 = u3 * fbar3 / a
    mid, part = sweep("mid", e, b, bv2, w3)
    fbar2 = u2 * reduce_add(part)
    w2 = u2 * fbar2 / a
    gb1, part = sweep("bwd", e, br, r, w2)
    fbar1 = reduce_add(part)
    w1 = fbar1 / a
    pieces = routes(share, count)
    half, keeps, sends = mix(
        share, pieces, e, arch_points, (bv3, bv2, mid, br, vbr, gb1), (u3, w3, u2, w2, w1)
    )
    terms, (pot, arch_grad, new_pot) = scatter_sum(
        keeps, sends, pieces, count, part,
        lambda after: back(
            total_cols, half, new_points, arch_points, e, b, r, n, sq, bv2, bv3, mid, gb1, vbr, w1,
            alpha, u3, after
        ),
    )
    row_weight = 2.0 * (fbar3 + fbar2 + fbar1) - a
    new_grad = gradient(pieces, rows, row_weight, mine, terms)
    return (new_pot.reshape(-1), pot.reshape(-1), new_grad, arch_grad)


def solution(mesh):
    in_specs = (P("pairs", None), P(("pairs", "cols"), None), P("pairs"), P(("pairs", "cols")))
    out_specs = (
        P("pairs"),
        P(("pairs", "cols")),
        P(("pairs", "cols"), None),
        P(("pairs", "cols"), None),
    )
    return jax.shard_map(local, mesh=mesh, in_specs=in_specs, out_specs=out_specs, check_vma=False)
```

```python
import functools
import math
import jax
import jax.numpy as jnp
from jax import lax
from jax.experimental import pallas as pl
from jax.experimental.pallas import tpu as pltpu
from jax.sharding import PartitionSpec as P

EPSILON = 0.05
LOGK = math.log2(math.e) / EPSILON
LANES = 128
SUB = 8
VMEM = pltpu.VMEM
F32 = jnp.float32
BF16 = jnp.bfloat16


def params(mib=28):
    return pltpu.CompilerParams(vmem_limit_bytes=mib * 1024 * 1024)


def full(n):
    return [pl.BlockSpec(memory_space=VMEM)] * n


def column(row):
    return jnp.transpose(jnp.broadcast_to(row, (LANES, LANES)))


def lanes(x):
    return [x[:, l * LANES:(l + 1) * LANES] for l in range(x.shape[1] // LANES)]


def wide(x):
    return jnp.broadcast_to(x, (SUB, LANES))


def tree(op, xs):
    xs = list(xs)
    while len(xs) > 1:
        xs = [op(xs[i], xs[i + 1]) if i + 1 < len(xs) else xs[i] for i in range(0, len(xs), 2)]
    return xs[0]


def lane_sum(xs):
    return wide(jnp.sum(tree(jnp.add, xs), axis=1, keepdims=True))


def lane_max(xs):
    return wide(jnp.max(tree(jnp.maximum, xs), axis=1, keepdims=True))


def rows_of(i, n):
    return pl.ds(pl.multiple_of(i * n, n), n)


def scores_kernel(total_cols, share, x_hbm, y_hbm, mass_hbm, z_ref, b_ref, sq_ref, lse_ref, mine_ref,
                  cb_ref, x_ref, y_ref, mass_ref, sems):
    cols, width = y_ref.shape
    rows = x_ref.shape[0]
    step = 2 * LANES
    copies = [
        pltpu.make_async_copy(hbm, ref, sems.at[i])
        for i, (hbm, ref) in enumerate(((x_hbm, x_ref), (y_hbm, y_ref), (mass_hbm, mass_ref)))
    ]
    for copy in copies:
        copy.start()
    for copy in copies:
        copy.wait()
    for c in range(cols // LANES):
        s = pl.ds(c * LANES, LANES)
        b = column(mass_ref[:, s] * (1.0 / total_cols))
        b_ref[s, :] = b
        yf = y_ref[s, :].astype(F32)
        sq = jnp.sum(yf * yf, axis=1, keepdims=True) * (LOGK / width)
        sq = jnp.broadcast_to(sq, (LANES, LANES))
        sq_ref[s, :] = sq
        cb_ref[s, :] = jnp.log2(b) - sq
    many = 4

    def reduce_block(r):
        for l in range(step // LANES):
            ls = pl.ds(r * step + l * LANES, LANES)
            m = [None] * many
            for g in range(cols // SUB):
                s = pl.ds(g * SUB, SUB)
                v = z_ref[s, ls] + cb_ref[s, :]
                m[g % many] = v if m[g % many] is None else jnp.maximum(m[g % many], v)
            m = jnp.max(tree(jnp.maximum, m), axis=0, keepdims=True)
            mw = wide(m)
            t = [None] * many
            for g in range(cols // SUB):
                s = pl.ds(g * SUB, SUB)
                v = jnp.exp2(z_ref[s, ls] + cb_ref[s, :] - mw)
                t[g % many] = v if t[g % many] is None else t[g % many] + v
            lse_ref[:, ls] = m + jnp.log2(jnp.sum(tree(jnp.add, t), axis=0, keepdims=True))

    for r in range(rows // step):
        s = pl.ds(r * step, step)
        z_ref[:, s] = lax.dot_general(
            y_ref[...], x_ref[s, :], (((1,), (1,)), ((), ())), preferred_element_type=F32
        ) * (2.0 * LOGK / width)
        if r > 0:
            reduce_block(r - 1)
    reduce_block(rows // step - 1)
    first = pl.multiple_of(lax.axis_index("cols") * share, share)
    mine_ref[...] = x_ref[pl.ds(first, share), :].astype(F32)


def scores(new_points, arch_points, arch_mass, total_cols, share):
    rows, cols = new_points.shape[0], arch_points.shape[0]
    return pl.pallas_call(
        functools.partial(scores_kernel, total_cols, share),
        out_shape=(
            VMEM((cols, rows), F32),
            VMEM((cols, LANES), F32),
            VMEM((cols, LANES), F32),
            jax.ShapeDtypeStruct((1, rows), F32),
            VMEM((share, new_points.shape[1]), F32),
        ),
        in_specs=[pl.BlockSpec(memory_space=pltpu.HBM)] * 3,
        out_specs=tuple(full(5)),
        scratch_shapes=[
            pltpu.VMEM((cols, LANES), F32),
            pltpu.VMEM(new_points.shape, BF16),
            pltpu.VMEM(arch_points.shape, BF16),
            pltpu.VMEM((1, cols), F32),
            pltpu.SemaphoreType.DMA((3,)),
        ],
        compiler_params=params(50),
        name="scores",
    )(new_points, arch_points, arch_mass.reshape(1, cols))


CHUNK = 512


def groups(i):
    return [pl.ds(pl.multiple_of(i * CHUNK, CHUNK) + h * SUB, SUB) for h in range(CHUNK // SUB)]


def column_dots(e_ref, w, tmp_ref):
    def body(i, carry):
        for s in groups(i):
            tmp_ref[s, :] = tree(jnp.add, [a * c for a, c in zip(lanes(e_ref[s, :]), w)])
        return carry

    lax.fori_loop(0, e_ref.shape[0] // CHUNK, body, 0)


def row_sums(e_ref, c_ref, part_ref):
    def body(i, acc):
        for s in groups(i):
            c = c_ref[s, :]
            acc = [a + d * c for a, d in zip(acc, lanes(e_ref[s, :]))]
        return acc

    cols, rows = e_ref.shape
    acc = lax.fori_loop(0, cols // CHUNK, body, [jnp.zeros((SUB, LANES), F32)] * (rows // LANES))
    for l, a in enumerate(acc):
        part_ref[:, pl.ds(l * LANES, LANES)] = jnp.sum(a, axis=0, keepdims=True)


def spread(x, op):
    return jnp.broadcast_to(op(x, axis=1, keepdims=True), x.shape)


def plan_kernel(z_ref, b_ref, sq_ref, w_ref, e_ref, n_ref, r_ref, br_ref, vbr_ref, part_ref, tmp_ref):
    cols, rows = z_ref.shape
    w = [wide(a) for a in lanes(w_ref[...])]

    def top(i, carry):
        for s in groups(i):
            tmp_ref[s, :] = tree(jnp.maximum, [a + c for a, c in zip(lanes(z_ref[s, :]), w)])
        return carry

    lax.fori_loop(0, cols // CHUNK, top, 0)

    def spread_top(i, carry):
        s = rows_of(i, CHUNK)
        n_ref[s, :] = spread(tmp_ref[s, :], jnp.max)
        return carry

    lax.fori_loop(0, cols // CHUNK, spread_top, 0)

    def powers(i, carry):
        for s in groups(i):
            n = n_ref[s, :]
            e = [jnp.exp2(a + c - n) for a, c in zip(lanes(z_ref[s, :]), w)]
            for l, a in enumerate(e):
                e_ref[s, pl.ds(l * LANES, LANES)] = a
            tmp_ref[s, :] = tree(jnp.add, e)
        return carry

    lax.fori_loop(0, cols // CHUNK, powers, 0)

    def scale(i, carry):
        s = rows_of(i, CHUNK)
        t = spread(tmp_ref[s, :], jnp.sum)
        r = 1.0 / t
        br = b_ref[s, :] * r
        r_ref[s, :] = r
        br_ref[s, :] = br
        vbr_ref[s, :] = br * jnp.exp2(n_ref[s, :] + jnp.log2(t) - sq_ref[s, :])
        return carry

    lax.fori_loop(0, cols // CHUNK, scale, 0)
    row_sums(e_ref, br_ref, part_ref)


def plan(z, b, sq, w):
    cols, rows = z.shape
    return pl.pallas_call(
        plan_kernel,
        out_shape=(VMEM((cols, rows), F32),) + (VMEM((cols, LANES), F32),) * 4
        + (jax.ShapeDtypeStruct((1, rows), F32),),
        in_specs=full(4),
        out_specs=tuple(full(6)),
        scratch_shapes=[pltpu.VMEM((cols, LANES), F32)],
        input_output_aliases={0: 0},
        compiler_params=params(8),
        name="plan",
    )(z, b, sq, w)


def sweep_kernel(kind, e_ref, b_ref, *refs):
    cols, rows = e_ref.shape
    more = refs[:-4]
    w_ref, c_ref, part_ref, tmp_ref = refs[-4:]
    column_dots(e_ref, [wide(a) for a in lanes(w_ref[...])], tmp_ref)

    def weigh(i, carry):
        s = rows_of(i, CHUNK)
        t = spread(tmp_ref[s, :], jnp.sum)
        b = b_ref[s, :]
        if kind == "fwd":
            c = b / t
        elif kind == "mid":
            v = more[0][s, :]
            c = v * v * t / b
        else:
            c = b * t * more[0][s, :]
        c_ref[s, :] = c
        return carry

    lax.fori_loop(0, cols // CHUNK, weigh, 0)
    row_sums(e_ref, c_ref, part_ref)


def sweep(kind, e, b, *more):
    cols, rows = e.shape
    return pl.pallas_call(
        functools.partial(sweep_kernel, kind),
        out_shape=(VMEM((cols, LANES), F32), jax.ShapeDtypeStruct((1, rows), F32)),
        in_specs=full(2 + len(more)),
        out_specs=tuple(full(2)),
        scratch_shapes=[pltpu.VMEM((cols, LANES), F32)],
        compiler_params=params(8),
        name="sweep_" + kind,
    )(e, b, *more)


def mix_kernel(share, pieces, e_ref, y_ref, *refs):
    c_refs, r_refs = refs[:6], refs[6:11]
    half_ref, (prod_ref, left_ref, right_ref) = refs[11], refs[-3:]
    send_refs = refs[12:-3]
    cols, rows = e_ref.shape
    pair = 2 * share
    me = lax.axis_index("cols")
    core = me % 2
    entry = lax.broadcasted_iota(jnp.int32, (SUB, LANES), 1)
    for g in range(cols // (2 * SUB)):
        outs = []
        for h in range(2):
            s = pl.ds(g * 2 * SUB + h * SUB, SUB)
            outs.append(split_parts([ref[s, :] for ref in c_refs], entry, LEFT))
        left_ref[pl.ds(g * 2 * SUB, 2 * SUB), :] = jnp.concatenate(outs, axis=0).astype(BF16)
    for l in range(rows // LANES):
        ls = pl.ds(l * LANES, LANES)
        r = [wide(ref[:, ls]) for ref in r_refs] + [jnp.ones((SUB, LANES), F32)]
        for g in range(LANES // (2 * SUB)):
            outs = []
            for h in range(2):
                at = lax.broadcasted_iota(jnp.int32, (SUB, LANES), 0) + (2 * g + h) * SUB
                outs.append(split_parts(r, at, RIGHT) if (2 * g + h) * SUB < 36 else jnp.zeros((SUB, LANES), F32))
            right_ref[pl.ds(g * 2 * SUB, 2 * SUB), ls] = jnp.concatenate(outs, axis=0).astype(BF16)
    for p in range(rows // pair):
        lo = pl.multiple_of(((me // 2) ^ p) * pair, pair)
        block = pl.ds(lo, pair)
        for g in range(cols // MIX):
            s = pl.ds(g * MIX, MIX)
            scale = jnp.dot(left_ref[s, :], right_ref[:, block], preferred_element_type=F32)
            half_ref[s, block] = (e_ref[s, block] * scale).astype(BF16)
        if p % 2:
            products(share, pieces, p - 1, 1 - core, half_ref, y_ref, prod_ref, send_refs)


def products(share, pieces, p, side, half_ref, y_ref, prod_ref, out_refs):
    me = lax.axis_index("cols")
    pair = 2 * share
    split = share % LANES == 0
    size = share if split else pair
    blocks = []
    for q in range(2):
        lo = ((me // 2) ^ (p + q)) * pair + (side * share if split else 0)
        blocks.append(half_ref[:, pl.ds(pl.multiple_of(lo, LANES), size)])
    slot = p // 2 % 2
    prod_ref[slot] = lax.dot_general(
        jnp.concatenate(blocks, axis=1), y_ref[...], (((0,), (0,)), ((), ())),
        preferred_element_type=F32,
    )
    for q in range(2):
        at = q * size + (0 if split else side * share)
        for ref, (n, bits) in zip(out_refs, pieces):
            ref[spot(p + q, bits)] = prod_ref[slot, pl.ds(pl.multiple_of(at, SUB), n), :]
            at = at + n


def keep_kernel(share, pieces, half_ref, y_ref, *refs):
    core = lax.axis_index("cols") % 2
    for p in range(0, half_ref.shape[1] // (2 * share), 2):
        products(share, pieces, p, core, half_ref, y_ref, refs[-1], refs[:-1])


LEFT = (0, 0, 1, 0, 1, 2)
RIGHT = (0, 1, 0, 2, 1, 0)
MIX = 256


def split_parts(values, entry, which):
    x = jnp.zeros_like(values[0])
    for t, v in enumerate(values):
        x = jnp.where((entry >= 6 * t) & (entry < 6 * t + 6), v, x)
    first = x.astype(BF16).astype(F32)
    rest = x - first
    second = rest.astype(BF16).astype(F32)
    part = sum(jnp.where(entry % 6 == q, w, 0) for q, w in enumerate(which))
    return jnp.where(part == 0, first, jnp.where(part == 1, second, rest - second))


def spot(p, bits):
    return sum(bool(2 * p & k) << i for i, k in enumerate(reversed(bits)))


def product_shapes(share, pieces, rows, width):
    out = [jax.ShapeDtypeStruct((rows // (2 * share), n, width), F32) for n, _ in pieces]
    size = share if share % LANES == 0 else 2 * share
    return out, pltpu.VMEM((2, 2 * size, width), F32)


def mix(share, pieces, e, y, columns, weights):
    cols, rows = e.shape
    out, scratch = product_shapes(share, pieces, rows, y.shape[1])
    half, *sends = pl.pallas_call(
        functools.partial(mix_kernel, share, pieces),
        out_shape=(VMEM((cols, rows), BF16), *out),
        in_specs=full(13),
        out_specs=tuple(full(1 + len(out))),
        scratch_shapes=[
            scratch,
            pltpu.VMEM((cols, LANES), BF16),
            pltpu.VMEM((LANES, rows), BF16),
        ],
        compiler_params=params(16),
        name="mix",
    )(e, y, *columns, *weights)
    return half, sends


def keep(share, pieces, half, y):
    out, scratch = product_shapes(share, pieces, half.shape[1], y.shape[1])
    return pl.pallas_call(
        functools.partial(keep_kernel, share, pieces),
        out_shape=tuple(out),
        in_specs=full(2),
        out_specs=tuple(full(len(out))),
        scratch_shapes=[scratch],
        compiler_params=params(16),
        name="keep",
    )(half, y)


def back_kernel(total_cols, half_ref, x_ref, y_ref, e_ref, b_ref, r_ref, n_ref, sq_ref, bv2_ref,
                bv3_ref, mid_ref, gb1_ref, vbr_ref, w_ref, alpha_ref, u3_ref, after_ref, pot_ref, arch_ref,
                new_ref, tmp_ref):
    del after_ref
    cols, rows = e_ref.shape
    width = y_ref.shape[1]
    column_dots(e_ref, [wide(a) for a in lanes(w_ref[...])], tmp_ref)
    step = 256
    for j in range(cols // step):
        s = pl.ds(j * step, step)
        b = b_ref[s, :]
        gb0 = vbr_ref[s, :] * spread(tmp_ref[s, :], jnp.sum)
        gb2 = mid_ref[s, :] * b / bv2_ref[s, :]
        tr = b + 2.0 * (gb2 + gb1_ref[s, :] / r_ref[s, :]) + gb0
        back = jnp.dot(half_ref[s, :], x_ref[...], preferred_element_type=F32)
        for l in range(width // LANES):
            ls = slice(l * LANES, (l + 1) * LANES)
            arch_ref[s, ls] = total_cols * (tr * y_ref[s, ls].astype(F32) - back[:, ls])
    for c in range(cols // LANES):
        s = pl.ds(c * LANES, LANES)
        pot = (sq_ref[s, :] - n_ref[s, :] + jnp.log2(bv3_ref[s, :] / b_ref[s, :])) * (1.0 / LOGK)
        pot_ref[:, s] = jnp.transpose(pot)[0:1, :]
    ones = jnp.ones((SUB, width), BF16)
    for i in range(rows // step):
        s = pl.ds(i * step, step)
        xf = x_ref[s, :].astype(F32)
        square = xf * xf
        high = square.astype(BF16)
        low = (square - high.astype(F32)).astype(BF16)
        sq = sum(
            lax.dot_general(ones, v, (((1,), (1,)), ((), ())), preferred_element_type=F32)
            for v in (high, low)
        )[0:1, :] * (LOGK / width)
        new_ref[:, s] = (alpha_ref[:, s] + jnp.log2(u3_ref[:, s]) + sq) * (1.0 / LOGK)


def back(total_cols, half, x, y, *rest):
    cols, rows = half.shape
    width = y.shape[1]
    return pl.pallas_call(
        functools.partial(back_kernel, float(total_cols)),
        out_shape=(
            jax.ShapeDtypeStruct((1, cols), F32),
            jax.ShapeDtypeStruct((cols, width), F32),
            jax.ShapeDtypeStruct((1, rows), F32),
        ),
        in_specs=full(2 + len(rest)) + [pl.BlockSpec(memory_space=pl.ANY)],
        out_specs=tuple(full(3)),
        scratch_shapes=[pltpu.VMEM((cols, LANES), F32)],
        compiler_params=params(16),
        cost_estimate=pl.CostEstimate(
            flops=2 * cols * rows * width, bytes_accessed=16 * 1024 * 1024, transcendentals=0
        ),
        name="back",
    )(half, x, y, *rest)


def swap(v, k, count):
    return lax.ppermute(v, "cols", [(i, i ^ k) for i in range(count)])


def fold_kernel(keep_ref, got_ref, after_ref, stay_ref, away_ref):
    del after_ref
    half = keep_ref.shape[0] // 2
    for i in range(half):
        stay_ref[i] = keep_ref[i] + got_ref[i]
        away_ref[i] = keep_ref[half + i] + got_ref[half + i]


def fold(keep, got, after):
    blocks, n, width = keep.shape
    return pl.pallas_call(
        fold_kernel,
        out_shape=(jax.ShapeDtypeStruct((blocks // 2, n, width), F32),) * 2,
        in_specs=full(2) + [pl.BlockSpec(memory_space=pl.ANY)],
        out_specs=tuple(full(2)),
        compiler_params=params(8),
        name="fold",
    )(keep, got, after)


def scatter_sum(keeps, sends, pieces, count, after, meanwhile):
    keeps = list(keeps)
    gots = [swap(send, 1, count) for send in sends]

    def advance(i, step, after):
        keeps[i], away = fold(keeps[i], gots[i], after)
        gots[i] = swap(away, pieces[i][1][step], count)
        return away

    steps = count.bit_length() - 2
    other = None
    for t in range(steps + 1):
        turn = [(0, t), (1, t), (2, t)] if t == 0 else [(2, t), (0, t)] + [(1, t - 1)] * (t > 1)
        for i, step in turn:
            if step < steps:
                after = advance(i, step, after)
        if t == 0:
            other = meanwhile(after)
            after = other[0]
    return [x[0] for pair in zip(keeps, gots) for x in pair], other


def gradient_kernel(pieces, scale, *refs):
    weight_ref, mine_ref = refs[:2]
    terms, (out_ref, col_ref) = refs[2:-2], refs[-2:]
    share, width = mine_ref.shape
    pair = 2 * share
    me = lax.axis_index("cols")
    lo = pl.multiple_of((me // 2) * pair, pair)
    for l in range(pair // LANES):
        at = pl.multiple_of(lo + l * LANES, LANES)
        col_ref[pl.ds(l * LANES, LANES), :] = column(weight_ref[:, pl.ds(at, LANES)])
    at = 0
    for i, (n, _) in enumerate(pieces):
        col = col_ref[pl.ds(pl.multiple_of((me % 2) * share + at, 8), n), :]
        for l in range(width // LANES):
            ls = pl.ds(l * LANES, LANES)
            out_ref[pl.ds(at, n), ls] = scale * (
                col * mine_ref[pl.ds(at, n), ls] - (terms[2 * i][:, ls] + terms[2 * i + 1][:, ls])
            )
        at += n


def gradient(pieces, scale, weight, mine, terms):
    share, width = mine.shape
    return pl.pallas_call(
        functools.partial(gradient_kernel, pieces, float(scale)),
        out_shape=jax.ShapeDtypeStruct((share, width), F32),
        in_specs=full(2 + len(terms)),
        out_specs=full(1)[0],
        scratch_shapes=[pltpu.VMEM((2 * share, LANES), F32)],
        compiler_params=params(8),
        name="gradient",
    )(weight, mine, *terms)


def combine(x, count, join):
    k = 1
    while k < count:
        if 4 * k <= count:
            x = join([x] + [swap(x, j * k, count) for j in (1, 2, 3)])
            k *= 4
        else:
            x = join([x, swap(x, k, count)])
            k *= 2
    return x


def add_join(xs):
    return tree(jnp.add, xs)


def lse_join(xs):
    m = tree(jnp.maximum, xs)
    return m + jnp.log2(tree(jnp.add, [jnp.exp2(x - m) for x in xs]))


def routes(share, count):
    bits = [1 << i for i in range(1, count.bit_length() - 1)]
    units = share // SUB
    first = units * 6 // 16
    last = units - 2 * first
    return [(first * SUB, bits), (first * SUB, bits), (last * SUB, bits[1:] + bits[:1])]


def local(new_points, arch_points, new_mass, arch_mass):
    rows = new_points.shape[0]
    count = lax.axis_size("cols")
    assert count & (count - 1) == 0
    reduce_add = functools.partial(combine, count=count, join=add_join)
    reduce_lse = functools.partial(combine, count=count, join=lse_join)
    total_cols = arch_points.shape[0] * count
    share = rows // count
    a = (new_mass / rows).reshape(1, rows)

    z, b, sq, lse, mine = scores(new_points, arch_points, arch_mass, total_cols, share)
    alpha = -reduce_lse(lse)
    e, n, r, br, vbr, part = plan(z, b, sq, jnp.log2(a) + alpha)
    u2 = a / reduce_add(part)
    bv2, part = sweep("fwd", e, b, u2)
    u3 = a / reduce_add(part)
    bv3, part = sweep("fwd", e, b, u3)
    fbar3 = a + u3 * reduce_add(part)
    w3 = u3 * fbar3 / a
    mid, part = sweep("mid", e, b, bv2, w3)
    fbar2 = u2 * reduce_add(part)
    w2 = u2 * fbar2 / a
    gb1, part = sweep("bwd", e, br, r, w2)
    fbar1 = reduce_add(part)
    w1 = fbar1 / a
    pieces = routes(share, count)
    half, sends = mix(
        share, pieces, e, arch_points, (bv3, bv2, mid, br, vbr, gb1), (u3, w3, u2, w2, w1)
    )
    keeps = keep(share, pieces, half, arch_points)
    terms, (pot, arch_grad, new_pot) = scatter_sum(
        keeps, sends, pieces, count, part,
        lambda after: back(
            total_cols, half, new_points, arch_points, e, b, r, n, sq, bv2, bv3, mid, gb1, vbr, w1,
            alpha, u3, after
        ),
    )
    row_weight = 2.0 * (fbar3 + fbar2 + fbar1) - a
    new_grad = gradient(pieces, rows, row_weight, mine, terms)
    return (new_pot.reshape(-1), pot.reshape(-1), new_grad, arch_grad)


def solution(mesh):
    in_specs = (P("pairs", None), P(("pairs", "cols"), None), P("pairs"), P(("pairs", "cols")))
    out_specs = (
        P("pairs"),
        P(("pairs", "cols")),
        P(("pairs", "cols"), None),
        P(("pairs", "cols"), None),
    )
    return jax.shard_map(local, mesh=mesh, in_specs=in_specs, out_specs=out_specs, check_vma=False)
```

```python
import functools
import math
import jax
import jax.numpy as jnp
from jax import lax
from jax.experimental import pallas as pl
from jax.experimental.pallas import tpu as pltpu
from jax.sharding import PartitionSpec as P

EPSILON = 0.05
LOGK = math.log2(math.e) / EPSILON
LANES = 128
SUB = 8
VMEM = pltpu.VMEM
F32 = jnp.float32
BF16 = jnp.bfloat16


def params(mib=28):
    return pltpu.CompilerParams(vmem_limit_bytes=mib * 1024 * 1024)


def full(n):
    return [pl.BlockSpec(memory_space=VMEM)] * n


def column(row):
    return jnp.transpose(jnp.broadcast_to(row, (LANES, LANES)))


def lanes(x):
    return [x[:, l * LANES:(l + 1) * LANES] for l in range(x.shape[1] // LANES)]


def wide(x):
    return jnp.broadcast_to(x, (SUB, LANES))


def tree(op, xs):
    xs = list(xs)
    while len(xs) > 1:
        xs = [op(xs[i], xs[i + 1]) if i + 1 < len(xs) else xs[i] for i in range(0, len(xs), 2)]
    return xs[0]


def lane_sum(xs):
    return wide(jnp.sum(tree(jnp.add, xs), axis=1, keepdims=True))


def lane_max(xs):
    return wide(jnp.max(tree(jnp.maximum, xs), axis=1, keepdims=True))


def rows_of(i, n):
    return pl.ds(pl.multiple_of(i * n, n), n)


def scores_kernel(total_cols, share, x_hbm, y_hbm, mass_hbm, z_ref, b_ref, sq_ref, lse_ref, mine_ref,
                  cb_ref, x_ref, y_ref, mass_ref, sems):
    cols, width = y_ref.shape
    rows = x_ref.shape[0]
    step = 2 * LANES
    copies = [
        pltpu.make_async_copy(hbm, ref, sems.at[i])
        for i, (hbm, ref) in enumerate(((x_hbm, x_ref), (y_hbm, y_ref), (mass_hbm, mass_ref)))
    ]
    for copy in copies:
        copy.start()
    for copy in copies:
        copy.wait()
    for c in range(cols // LANES):
        s = pl.ds(c * LANES, LANES)
        b = column(mass_ref[:, s] * (1.0 / total_cols))
        b_ref[s, :] = b
        yf = y_ref[s, :].astype(F32)
        sq = jnp.sum(yf * yf, axis=1, keepdims=True) * (LOGK / width)
        sq = jnp.broadcast_to(sq, (LANES, LANES))
        sq_ref[s, :] = sq
        cb_ref[s, :] = jnp.log2(b) - sq
    many = 4

    def reduce_block(r):
        for l in range(step // LANES):
            ls = pl.ds(r * step + l * LANES, LANES)
            m = [None] * many
            for g in range(cols // SUB):
                s = pl.ds(g * SUB, SUB)
                v = z_ref[s, ls] + cb_ref[s, :]
                m[g % many] = v if m[g % many] is None else jnp.maximum(m[g % many], v)
            m = jnp.max(tree(jnp.maximum, m), axis=0, keepdims=True)
            mw = wide(m)
            t = [None] * many
            for g in range(cols // SUB):
                s = pl.ds(g * SUB, SUB)
                v = jnp.exp2(z_ref[s, ls] + cb_ref[s, :] - mw)
                t[g % many] = v if t[g % many] is None else t[g % many] + v
            lse_ref[:, ls] = m + jnp.log2(jnp.sum(tree(jnp.add, t), axis=0, keepdims=True))

    for r in range(rows // step):
        s = pl.ds(r * step, step)
        z_ref[:, s] = lax.dot_general(
            y_ref[...], x_ref[s, :], (((1,), (1,)), ((), ())), preferred_element_type=F32
        ) * (2.0 * LOGK / width)
        if r > 0:
            reduce_block(r - 1)
    reduce_block(rows // step - 1)
    first = pl.multiple_of(lax.axis_index("cols") * share, share)
    mine_ref[...] = x_ref[pl.ds(first, share), :].astype(F32)


def scores(new_points, arch_points, arch_mass, total_cols, share):
    rows, cols = new_points.shape[0], arch_points.shape[0]
    return pl.pallas_call(
        functools.partial(scores_kernel, total_cols, share),
        out_shape=(
            VMEM((cols, rows), F32),
            VMEM((cols, LANES), F32),
            VMEM((cols, LANES), F32),
            VMEM((1, rows), F32),
            VMEM((share, new_points.shape[1]), F32),
        ),
        in_specs=[pl.BlockSpec(memory_space=pltpu.HBM)] * 3,
        out_specs=tuple(full(5)),
        scratch_shapes=[
            pltpu.VMEM((cols, LANES), F32),
            pltpu.VMEM(new_points.shape, BF16),
            pltpu.VMEM(arch_points.shape, BF16),
            pltpu.VMEM((1, cols), F32),
            pltpu.SemaphoreType.DMA((3,)),
        ],
        compiler_params=params(50),
        name="scores",
    )(new_points, arch_points, arch_mass.reshape(1, cols))


CHUNK = 512


def groups(i):
    return [pl.ds(pl.multiple_of(i * CHUNK, CHUNK) + h * SUB, SUB) for h in range(CHUNK // SUB)]


def column_dots(e_ref, w, tmp_ref):
    def body(i, carry):
        for s in groups(i):
            tmp_ref[s, :] = tree(jnp.add, [a * c for a, c in zip(lanes(e_ref[s, :]), w)])
        return carry

    lax.fori_loop(0, e_ref.shape[0] // CHUNK, body, 0)


def row_sums(e_ref, c_ref, part_ref):
    def body(i, acc):
        for s in groups(i):
            c = c_ref[s, :]
            acc = [a + d * c for a, d in zip(acc, lanes(e_ref[s, :]))]
        return acc

    cols, rows = e_ref.shape
    acc = lax.fori_loop(0, cols // CHUNK, body, [jnp.zeros((SUB, LANES), F32)] * (rows // LANES))
    for l, a in enumerate(acc):
        part_ref[:, pl.ds(l * LANES, LANES)] = jnp.sum(a, axis=0, keepdims=True)


def spread(x, op):
    return jnp.broadcast_to(op(x, axis=1, keepdims=True), x.shape)


def plan_kernel(z_ref, b_ref, sq_ref, w_ref, e_ref, n_ref, r_ref, br_ref, vbr_ref, part_ref, tmp_ref):
    cols, rows = z_ref.shape
    w = [wide(a) for a in lanes(w_ref[...])]

    def top(i, carry):
        for s in groups(i):
            tmp_ref[s, :] = tree(jnp.maximum, [a + c for a, c in zip(lanes(z_ref[s, :]), w)])
        return carry

    lax.fori_loop(0, cols // CHUNK, top, 0)

    def spread_top(i, carry):
        s = rows_of(i, CHUNK)
        n_ref[s, :] = spread(tmp_ref[s, :], jnp.max)
        return carry

    lax.fori_loop(0, cols // CHUNK, spread_top, 0)

    def powers(i, carry):
        for s in groups(i):
            n = n_ref[s, :]
            e = [jnp.exp2(a + c - n) for a, c in zip(lanes(z_ref[s, :]), w)]
            for l, a in enumerate(e):
                e_ref[s, pl.ds(l * LANES, LANES)] = a
            tmp_ref[s, :] = tree(jnp.add, e)
        return carry

    lax.fori_loop(0, cols // CHUNK, powers, 0)

    def scale(i, carry):
        s = rows_of(i, CHUNK)
        t = spread(tmp_ref[s, :], jnp.sum)
        r = 1.0 / t
        br = b_ref[s, :] * r
        r_ref[s, :] = r
        br_ref[s, :] = br
        vbr_ref[s, :] = br * jnp.exp2(n_ref[s, :] + jnp.log2(t) - sq_ref[s, :])
        return carry

    lax.fori_loop(0, cols // CHUNK, scale, 0)
    row_sums(e_ref, br_ref, part_ref)


def plan(z, b, sq, w):
    cols, rows = z.shape
    return pl.pallas_call(
        plan_kernel,
        out_shape=(VMEM((cols, rows), F32),) + (VMEM((cols, LANES), F32),) * 4
        + (jax.ShapeDtypeStruct((1, rows), F32),),
        in_specs=full(4),
        out_specs=tuple(full(6)),
        scratch_shapes=[pltpu.VMEM((cols, LANES), F32)],
        input_output_aliases={0: 0},
        compiler_params=params(8),
        name="plan",
    )(z, b, sq, w)


def sweep_kernel(kind, e_ref, b_ref, *refs):
    cols, rows = e_ref.shape
    more = refs[:-4]
    w_ref, c_ref, part_ref, tmp_ref = refs[-4:]
    column_dots(e_ref, [wide(a) for a in lanes(w_ref[...])], tmp_ref)

    def weigh(i, carry):
        s = rows_of(i, CHUNK)
        t = spread(tmp_ref[s, :], jnp.sum)
        b = b_ref[s, :]
        if kind == "fwd":
            c = b / t
        elif kind == "mid":
            v = more[0][s, :]
            c = v * v * t / b
        else:
            c = b * t * more[0][s, :]
        c_ref[s, :] = c
        return carry

    lax.fori_loop(0, cols // CHUNK, weigh, 0)
    row_sums(e_ref, c_ref, part_ref)


def sweep(kind, e, b, *more):
    cols, rows = e.shape
    return pl.pallas_call(
        functools.partial(sweep_kernel, kind),
        out_shape=(VMEM((cols, LANES), F32), jax.ShapeDtypeStruct((1, rows), F32)),
        in_specs=full(2 + len(more)),
        out_specs=tuple(full(2)),
        scratch_shapes=[pltpu.VMEM((cols, LANES), F32)],
        compiler_params=params(8),
        name="sweep_" + kind,
    )(e, b, *more)


def mix_kernel(share, pieces, e_ref, y_ref, *refs):
    c_refs, r_refs = refs[:6], refs[6:11]
    half_ref, (prod_ref, left_ref, right_ref) = refs[11], refs[-3:]
    send_refs = refs[12:-3]
    cols, rows = e_ref.shape
    pair = 2 * share
    me = lax.axis_index("cols")
    core = me % 2
    entry = lax.broadcasted_iota(jnp.int32, (SUB, LANES), 1)
    for g in range(cols // (2 * SUB)):
        outs = []
        for h in range(2):
            s = pl.ds(g * 2 * SUB + h * SUB, SUB)
            outs.append(split_parts([ref[s, :] for ref in c_refs], entry, LEFT))
        left_ref[pl.ds(g * 2 * SUB, 2 * SUB), :] = jnp.concatenate(outs, axis=0).astype(BF16)
    for l in range(rows // LANES):
        ls = pl.ds(l * LANES, LANES)
        r = [wide(ref[:, ls]) for ref in r_refs] + [jnp.ones((SUB, LANES), F32)]
        for g in range(LANES // (2 * SUB)):
            outs = []
            for h in range(2):
                at = lax.broadcasted_iota(jnp.int32, (SUB, LANES), 0) + (2 * g + h) * SUB
                outs.append(split_parts(r, at, RIGHT) if (2 * g + h) * SUB < 36 else jnp.zeros((SUB, LANES), F32))
            right_ref[pl.ds(g * 2 * SUB, 2 * SUB), ls] = jnp.concatenate(outs, axis=0).astype(BF16)
    for p in range(rows // pair):
        lo = pl.multiple_of(((me // 2) ^ p) * pair, pair)
        block = pl.ds(lo, pair)
        for g in range(cols // MIX):
            s = pl.ds(g * MIX, MIX)
            scale = jnp.dot(left_ref[s, :], right_ref[:, block], preferred_element_type=F32)
            half_ref[s, block] = (e_ref[s, block] * scale).astype(BF16)
        if p % 2:
            products(share, pieces, p - 1, 1 - core, half_ref, y_ref, prod_ref, send_refs)


def products(share, pieces, p, side, half_ref, y_ref, prod_ref, out_refs):
    me = lax.axis_index("cols")
    pair = 2 * share
    split = share % LANES == 0
    size = share if split else pair
    blocks = []
    for q in range(2):
        lo = ((me // 2) ^ (p + q)) * pair + (side * share if split else 0)
        blocks.append(half_ref[:, pl.ds(pl.multiple_of(lo, LANES), size)])
    slot = p // 2 % 2
    prod_ref[slot] = lax.dot_general(
        jnp.concatenate(blocks, axis=1), y_ref[...], (((0,), (0,)), ((), ())),
        preferred_element_type=F32,
    )
    for q in range(2):
        at = q * size + (0 if split else side * share)
        for ref, (n, bits) in zip(out_refs, pieces):
            ref[spot(p + q, bits)] = prod_ref[slot, pl.ds(pl.multiple_of(at, SUB), n), :]
            at = at + n


def keep_kernel(share, pieces, half_ref, y_ref, *refs):
    core = lax.axis_index("cols") % 2
    for p in range(0, half_ref.shape[1] // (2 * share), 2):
        products(share, pieces, p, core, half_ref, y_ref, refs[-1], refs[:-1])


LEFT = (0, 0, 1, 0, 1, 2)
RIGHT = (0, 1, 0, 2, 1, 0)
MIX = 256


def split_parts(values, entry, which):
    x = jnp.zeros_like(values[0])
    for t, v in enumerate(values):
        x = jnp.where((entry >= 6 * t) & (entry < 6 * t + 6), v, x)
    first = x.astype(BF16).astype(F32)
    rest = x - first
    second = rest.astype(BF16).astype(F32)
    part = sum(jnp.where(entry % 6 == q, w, 0) for q, w in enumerate(which))
    return jnp.where(part == 0, first, jnp.where(part == 1, second, rest - second))


def spot(p, bits):
    return sum(bool(2 * p & k) << i for i, k in enumerate(reversed(bits)))


def product_shapes(share, pieces, rows, width):
    out = [jax.ShapeDtypeStruct((rows // (2 * share), n, width), F32) for n, _ in pieces]
    size = share if share % LANES == 0 else 2 * share
    return out, pltpu.VMEM((2, 2 * size, width), F32)


def mix(share, pieces, e, y, columns, weights):
    cols, rows = e.shape
    out, scratch = product_shapes(share, pieces, rows, y.shape[1])
    half, *sends = pl.pallas_call(
        functools.partial(mix_kernel, share, pieces),
        out_shape=(VMEM((cols, rows), BF16), *out),
        in_specs=full(13),
        out_specs=tuple(full(1 + len(out))),
        scratch_shapes=[
            scratch,
            pltpu.VMEM((cols, LANES), BF16),
            pltpu.VMEM((LANES, rows), BF16),
        ],
        compiler_params=params(16),
        name="mix",
    )(e, y, *columns, *weights)
    return half, sends


def keep(share, pieces, half, y):
    out, scratch = product_shapes(share, pieces, half.shape[1], y.shape[1])
    return pl.pallas_call(
        functools.partial(keep_kernel, share, pieces),
        out_shape=tuple(out),
        in_specs=full(2),
        out_specs=tuple(full(len(out))),
        scratch_shapes=[scratch],
        compiler_params=params(16),
        name="keep",
    )(half, y)


def back_kernel(total_cols, half_ref, x_ref, y_ref, e_ref, b_ref, r_ref, n_ref, sq_ref, bv2_ref,
                bv3_ref, mid_ref, gb1_ref, vbr_ref, w_ref, alpha_ref, u3_ref, weight_ref, mine_ref, after_ref,
                pot_ref, arch_ref, new_ref, base_ref, tmp_ref, col_ref):
    del after_ref
    share = mine_ref.shape[0]
    pair = 2 * share
    me = lax.axis_index("cols")
    lo = pl.multiple_of((me // 2) * pair, pair)
    for l in range(pair // LANES):
        at = pl.multiple_of(lo + l * LANES, LANES)
        col_ref[pl.ds(l * LANES, LANES), :] = column(weight_ref[:, pl.ds(at, LANES)])
    col = col_ref[pl.ds(pl.multiple_of((me % 2) * share, share), share), :]
    for l in range(mine_ref.shape[1] // LANES):
        ls = pl.ds(l * LANES, LANES)
        base_ref[:, ls] = col * mine_ref[:, ls]
    cols, rows = e_ref.shape
    width = y_ref.shape[1]
    column_dots(e_ref, [wide(a) for a in lanes(w_ref[...])], tmp_ref)
    step = 256
    for j in range(cols // step):
        s = pl.ds(j * step, step)
        b = b_ref[s, :]
        gb0 = vbr_ref[s, :] * spread(tmp_ref[s, :], jnp.sum)
        gb2 = mid_ref[s, :] * b / bv2_ref[s, :]
        tr = b + 2.0 * (gb2 + gb1_ref[s, :] / r_ref[s, :]) + gb0
        back = jnp.dot(half_ref[s, :], x_ref[...], preferred_element_type=F32)
        for l in range(width // LANES):
            ls = slice(l * LANES, (l + 1) * LANES)
            arch_ref[s, ls] = total_cols * (tr * y_ref[s, ls].astype(F32) - back[:, ls])
    for c in range(cols // LANES):
        s = pl.ds(c * LANES, LANES)
        pot = (sq_ref[s, :] - n_ref[s, :] + jnp.log2(bv3_ref[s, :] / b_ref[s, :])) * (1.0 / LOGK)
        pot_ref[:, s] = jnp.transpose(pot)[0:1, :]
    ones = jnp.ones((SUB, width), BF16)
    for i in range(rows // step):
        s = pl.ds(i * step, step)
        xf = x_ref[s, :].astype(F32)
        square = xf * xf
        high = square.astype(BF16)
        low = (square - high.astype(F32)).astype(BF16)
        sq = sum(
            lax.dot_general(ones, v, (((1,), (1,)), ((), ())), preferred_element_type=F32)
            for v in (high, low)
        )[0:1, :] * (LOGK / width)
        new_ref[:, s] = (alpha_ref[:, s] + jnp.log2(u3_ref[:, s]) + sq) * (1.0 / LOGK)


def back(total_cols, half, x, y, *rest, mine, after):
    cols, rows = half.shape
    width = y.shape[1]
    return pl.pallas_call(
        functools.partial(back_kernel, float(total_cols)),
        out_shape=(
            jax.ShapeDtypeStruct((1, cols), F32),
            jax.ShapeDtypeStruct((cols, width), F32),
            jax.ShapeDtypeStruct((1, rows), F32),
            VMEM(mine.shape, F32),
        ),
        in_specs=full(4 + len(rest)) + [pl.BlockSpec(memory_space=pl.ANY)],
        out_specs=tuple(full(4)),
        scratch_shapes=[
            pltpu.VMEM((cols, LANES), F32), pltpu.VMEM((2 * mine.shape[0], LANES), F32)
        ],
        compiler_params=params(16),
        cost_estimate=pl.CostEstimate(
            flops=2 * cols * rows * width, bytes_accessed=16 * 1024 * 1024, transcendentals=0
        ),
        name="back",
    )(half, x, y, *rest, mine, after)


def swap(v, k, count):
    return lax.ppermute(v, "cols", [(i, i ^ k) for i in range(count)])


def fold_kernel(keep_ref, got_ref, after_ref, stay_ref, away_ref):
    del after_ref
    half = keep_ref.shape[0] // 2
    for i in range(half):
        stay_ref[i] = keep_ref[i] + got_ref[i]
        away_ref[i] = keep_ref[half + i] + got_ref[half + i]


def fold(keep, got, after):
    blocks, n, width = keep.shape
    return pl.pallas_call(
        fold_kernel,
        out_shape=(jax.ShapeDtypeStruct((blocks // 2, n, width), F32),) * 2,
        in_specs=full(2) + [pl.BlockSpec(memory_space=pl.ANY)],
        out_specs=tuple(full(2)),
        compiler_params=params(8),
        name="fold",
    )(keep, got, after)


def scatter_sum(keeps, sends, pieces, count, after, meanwhile):
    keeps = list(keeps)
    gots = [swap(send, 1, count) for send in sends]

    def advance(i, step, after):
        keeps[i], away = fold(keeps[i], gots[i], after)
        gots[i] = swap(away, pieces[i][1][step], count)
        return away

    steps = count.bit_length() - 2
    other = None
    for t in range(steps + 1):
        turn = [(0, t), (1, t), (2, t)] if t == 0 else [(2, t), (0, t)] + [(1, t - 1)] * (t > 1)
        for i, step in turn:
            if step < steps:
                after = advance(i, step, after)
        if t == 0:
            other = meanwhile(after)
            after = other[-1]
    return [x[0] for pair in zip(keeps, gots) for x in pair], other


def gradient_kernel(pieces, scale, base_ref, *refs):
    terms, out_ref = refs[:-1], refs[-1]
    at = 0
    for i, (n, _) in enumerate(pieces):
        s = pl.ds(at, n)
        out_ref[s, :] = scale * (base_ref[s, :] - (terms[2 * i][...] + terms[2 * i + 1][...]))
        at += n


def gradient(pieces, scale, base, terms):
    return pl.pallas_call(
        functools.partial(gradient_kernel, pieces, float(scale)),
        out_shape=jax.ShapeDtypeStruct(base.shape, F32),
        in_specs=full(1 + len(terms)),
        out_specs=full(1)[0],
        compiler_params=params(8),
        name="gradient",
    )(base, *terms)


def combine(x, count, join):
    k = 1
    while k < count:
        if 4 * k <= count:
            x = join([x] + [swap(x, j * k, count) for j in (1, 2, 3)])
            k *= 4
        else:
            x = join([x, swap(x, k, count)])
            k *= 2
    return x


def add_join(xs):
    return tree(jnp.add, xs)


def lse_kernel(*refs):
    for l in range(refs[0].shape[1] // LANES):
        ls = pl.ds(l * LANES, LANES)
        xs = [ref[:, ls] for ref in refs[:-1]]
        m = tree(jnp.maximum, xs)
        refs[-1][:, ls] = m + jnp.log2(tree(jnp.add, [jnp.exp2(x - m) for x in xs]))


def lse_join(xs):
    return pl.pallas_call(
        lse_kernel,
        out_shape=jax.ShapeDtypeStruct(xs[0].shape, F32),
        in_specs=full(len(xs)),
        out_specs=full(1)[0],
        compiler_params=params(8),
        name="lse_join",
    )(*xs)


def routes(share, count):
    bits = [1 << i for i in range(1, count.bit_length() - 1)]
    units = share // SUB
    first = units * 6 // 16
    last = units - 2 * first
    return [(first * SUB, bits), (first * SUB, bits), (last * SUB, bits[1:] + bits[:1])]


def local(new_points, arch_points, new_mass, arch_mass):
    rows = new_points.shape[0]
    count = lax.axis_size("cols")
    assert count & (count - 1) == 0
    reduce_add = functools.partial(combine, count=count, join=add_join)
    reduce_lse = functools.partial(combine, count=count, join=lse_join)
    total_cols = arch_points.shape[0] * count
    share = rows // count
    a = (new_mass / rows).reshape(1, rows)

    z, b, sq, lse, mine = scores(new_points, arch_points, arch_mass, total_cols, share)
    alpha = -reduce_lse(lse)
    e, n, r, br, vbr, part = plan(z, b, sq, jnp.log2(a) + alpha)
    u2 = a / reduce_add(part)
    bv2, part = sweep("fwd", e, b, u2)
    u3 = a / reduce_add(part)
    bv3, part = sweep("fwd", e, b, u3)
    fbar3 = a + u3 * reduce_add(part)
    w3 = u3 * fbar3 / a
    mid, part = sweep("mid", e, b, bv2, w3)
    fbar2 = u2 * reduce_add(part)
    w2 = u2 * fbar2 / a
    gb1, part = sweep("bwd", e, br, r, w2)
    fbar1 = reduce_add(part)
    w1 = fbar1 / a
    pieces = routes(share, count)
    half, sends = mix(
        share, pieces, e, arch_points, (bv3, bv2, mid, br, vbr, gb1), (u3, w3, u2, w2, w1)
    )
    keeps = keep(share, pieces, half, arch_points)
    row_weight = 2.0 * (fbar3 + fbar2 + fbar1) - a
    terms, (pot, arch_grad, new_pot, base) = scatter_sum(
        keeps, sends, pieces, count, part,
        lambda after: back(
            total_cols, half, new_points, arch_points, e, b, r, n, sq, bv2, bv3, mid, gb1, vbr, w1,
            alpha, u3, row_weight, mine=mine, after=after
        ),
    )
    new_grad = gradient(pieces, rows, base, terms)
    return (new_pot.reshape(-1), pot.reshape(-1), new_grad, arch_grad)


def solution(mesh):
    in_specs = (P("pairs", None), P(("pairs", "cols"), None), P("pairs"), P(("pairs", "cols")))
    out_specs = (
        P("pairs"),
        P(("pairs", "cols")),
        P(("pairs", "cols"), None),
        P(("pairs", "cols"), None),
    )
    return jax.shard_map(local, mesh=mesh, in_specs=in_specs, out_specs=out_specs, check_vma=False)
```

```python
import functools
import math
import jax
import jax.numpy as jnp
from jax import lax
from jax.experimental import pallas as pl
from jax.experimental.pallas import tpu as pltpu
from jax.sharding import PartitionSpec as P

EPSILON = 0.05
LOGK = math.log2(math.e) / EPSILON
LANES = 128
SUB = 8
VMEM = pltpu.VMEM
F32 = jnp.float32
BF16 = jnp.bfloat16


def params(mib=28):
    return pltpu.CompilerParams(vmem_limit_bytes=mib * 1024 * 1024)


def full(n):
    return [pl.BlockSpec(memory_space=VMEM)] * n


def column(row):
    return jnp.transpose(jnp.broadcast_to(row, (LANES, LANES)))


def lanes(x):
    return [x[:, l * LANES:(l + 1) * LANES] for l in range(x.shape[1] // LANES)]


def wide(x):
    return jnp.broadcast_to(x, (SUB, LANES))


def tree(op, xs):
    xs = list(xs)
    while len(xs) > 1:
        xs = [op(xs[i], xs[i + 1]) if i + 1 < len(xs) else xs[i] for i in range(0, len(xs), 2)]
    return xs[0]


def lane_sum(xs):
    return wide(jnp.sum(tree(jnp.add, xs), axis=1, keepdims=True))


def lane_max(xs):
    return wide(jnp.max(tree(jnp.maximum, xs), axis=1, keepdims=True))


def rows_of(i, n):
    return pl.ds(pl.multiple_of(i * n, n), n)


def scores_kernel(total_cols, share, x_hbm, y_hbm, mass_hbm, z_ref, b_ref, sq_ref, lse_ref, mine_ref,
                  cb_ref, x_ref, y_ref, mass_ref, sems):
    cols, width = y_ref.shape
    rows = x_ref.shape[0]
    step = 2 * LANES
    copies = [
        pltpu.make_async_copy(hbm, ref, sems.at[i])
        for i, (hbm, ref) in enumerate(((mass_hbm, mass_ref), (y_hbm, y_ref), (x_hbm, x_ref)))
    ]
    for copy in copies:
        copy.start()
    copies[0].wait()
    copies[1].wait()
    for c in range(cols // LANES):
        s = pl.ds(c * LANES, LANES)
        b = column(mass_ref[:, s] * (1.0 / total_cols))
        b_ref[s, :] = b
        yf = y_ref[s, :].astype(F32)
        sq = jnp.sum(yf * yf, axis=1, keepdims=True) * (LOGK / width)
        sq = jnp.broadcast_to(sq, (LANES, LANES))
        sq_ref[s, :] = sq
        cb_ref[s, :] = jnp.log2(b) - sq
    copies[2].wait()
    many = 4

    def reduce_block(r):
        for l in range(step // LANES):
            ls = pl.ds(r * step + l * LANES, LANES)
            m = [None] * many
            for g in range(cols // SUB):
                s = pl.ds(g * SUB, SUB)
                v = z_ref[s, ls] + cb_ref[s, :]
                m[g % many] = v if m[g % many] is None else jnp.maximum(m[g % many], v)
            m = jnp.max(tree(jnp.maximum, m), axis=0, keepdims=True)
            mw = wide(m)
            t = [None] * many
            for g in range(cols // SUB):
                s = pl.ds(g * SUB, SUB)
                v = jnp.exp2(z_ref[s, ls] + cb_ref[s, :] - mw)
                t[g % many] = v if t[g % many] is None else t[g % many] + v
            lse_ref[:, ls] = m + jnp.log2(jnp.sum(tree(jnp.add, t), axis=0, keepdims=True))

    for r in range(rows // step):
        s = pl.ds(r * step, step)
        z_ref[:, s] = lax.dot_general(
            y_ref[...], x_ref[s, :], (((1,), (1,)), ((), ())), preferred_element_type=F32
        ) * (2.0 * LOGK / width)
        if r > 0:
            reduce_block(r - 1)
    reduce_block(rows // step - 1)
    first = pl.multiple_of(lax.axis_index("cols") * share, share)
    mine_ref[...] = x_ref[pl.ds(first, share), :].astype(F32)


def scores(new_points, arch_points, arch_mass, total_cols, share):
    rows, cols = new_points.shape[0], arch_points.shape[0]
    return pl.pallas_call(
        functools.partial(scores_kernel, total_cols, share),
        out_shape=(
            VMEM((cols, rows), F32),
            VMEM((cols, LANES), F32),
            VMEM((cols, LANES), F32),
            VMEM((1, rows), F32),
            VMEM((share, new_points.shape[1]), F32),
        ),
        in_specs=[pl.BlockSpec(memory_space=pltpu.HBM)] * 3,
        out_specs=tuple(full(5)),
        scratch_shapes=[
            pltpu.VMEM((cols, LANES), F32),
            pltpu.VMEM(new_points.shape, BF16),
            pltpu.VMEM(arch_points.shape, BF16),
            pltpu.VMEM((1, cols), F32),
            pltpu.SemaphoreType.DMA((3,)),
        ],
        compiler_params=params(50),
        name="scores",
    )(new_points, arch_points, arch_mass.reshape(1, cols))


CHUNK = 512


def groups(i):
    return [pl.ds(pl.multiple_of(i * CHUNK, CHUNK) + h * SUB, SUB) for h in range(CHUNK // SUB)]


def column_dots(e_ref, w, tmp_ref):
    def body(i, carry):
        for s in groups(i):
            tmp_ref[s, :] = tree(jnp.add, [a * c for a, c in zip(lanes(e_ref[s, :]), w)])
        return carry

    lax.fori_loop(0, e_ref.shape[0] // CHUNK, body, 0)


def row_sums(e_ref, c_ref, part_ref):
    def body(i, acc):
        for s in groups(i):
            c = c_ref[s, :]
            acc = [a + d * c for a, d in zip(acc, lanes(e_ref[s, :]))]
        return acc

    cols, rows = e_ref.shape
    acc = lax.fori_loop(0, cols // CHUNK, body, [jnp.zeros((SUB, LANES), F32)] * (rows // LANES))
    for l, a in enumerate(acc):
        part_ref[:, pl.ds(l * LANES, LANES)] = jnp.sum(a, axis=0, keepdims=True)


def spread(x, op):
    return jnp.broadcast_to(op(x, axis=1, keepdims=True), x.shape)


def plan_kernel(z_ref, b_ref, sq_ref, w_ref, e_ref, n_ref, r_ref, br_ref, vbr_ref, part_ref, tmp_ref):
    cols, rows = z_ref.shape
    w = [wide(a) for a in lanes(w_ref[...])]

    def top(i, carry):
        for s in groups(i):
            tmp_ref[s, :] = tree(jnp.maximum, [a + c for a, c in zip(lanes(z_ref[s, :]), w)])
        return carry

    lax.fori_loop(0, cols // CHUNK, top, 0)

    def spread_top(i, carry):
        s = rows_of(i, CHUNK)
        n_ref[s, :] = spread(tmp_ref[s, :], jnp.max)
        return carry

    lax.fori_loop(0, cols // CHUNK, spread_top, 0)

    def powers(i, carry):
        for s in groups(i):
            n = n_ref[s, :]
            e = [jnp.exp2(a + c - n) for a, c in zip(lanes(z_ref[s, :]), w)]
            for l, a in enumerate(e):
                e_ref[s, pl.ds(l * LANES, LANES)] = a
            tmp_ref[s, :] = tree(jnp.add, e)
        return carry

    lax.fori_loop(0, cols // CHUNK, powers, 0)

    def scale(i, carry):
        s = rows_of(i, CHUNK)
        t = spread(tmp_ref[s, :], jnp.sum)
        r = 1.0 / t
        br = b_ref[s, :] * r
        r_ref[s, :] = r
        br_ref[s, :] = br
        vbr_ref[s, :] = br * jnp.exp2(n_ref[s, :] + jnp.log2(t) - sq_ref[s, :])
        return carry

    lax.fori_loop(0, cols // CHUNK, scale, 0)
    row_sums(e_ref, br_ref, part_ref)


def plan(z, b, sq, w):
    cols, rows = z.shape
    return pl.pallas_call(
        plan_kernel,
        out_shape=(VMEM((cols, rows), F32),) + (VMEM((cols, LANES), F32),) * 4
        + (jax.ShapeDtypeStruct((1, rows), F32),),
        in_specs=full(4),
        out_specs=tuple(full(6)),
        scratch_shapes=[pltpu.VMEM((cols, LANES), F32)],
        input_output_aliases={0: 0},
        compiler_params=params(8),
        name="plan",
    )(z, b, sq, w)


def sweep_kernel(kind, e_ref, b_ref, *refs):
    cols, rows = e_ref.shape
    more = refs[:-4]
    w_ref, c_ref, part_ref, tmp_ref = refs[-4:]
    column_dots(e_ref, [wide(a) for a in lanes(w_ref[...])], tmp_ref)

    def weigh(i, carry):
        s = rows_of(i, CHUNK)
        t = spread(tmp_ref[s, :], jnp.sum)
        b = b_ref[s, :]
        if kind == "fwd":
            c = b / t
        elif kind == "mid":
            v = more[0][s, :]
            c = v * v * t / b
        else:
            c = b * t * more[0][s, :]
        c_ref[s, :] = c
        return carry

    lax.fori_loop(0, cols // CHUNK, weigh, 0)
    row_sums(e_ref, c_ref, part_ref)


def sweep(kind, e, b, *more):
    cols, rows = e.shape
    return pl.pallas_call(
        functools.partial(sweep_kernel, kind),
        out_shape=(VMEM((cols, LANES), F32), jax.ShapeDtypeStruct((1, rows), F32)),
        in_specs=full(2 + len(more)),
        out_specs=tuple(full(2)),
        scratch_shapes=[pltpu.VMEM((cols, LANES), F32)],
        compiler_params=params(8),
        name="sweep_" + kind,
    )(e, b, *more)


def mix_kernel(share, pieces, e_ref, y_ref, *refs):
    c_refs, r_refs = refs[:6], refs[6:11]
    half_ref, (prod_ref, left_ref, right_ref) = refs[11], refs[-3:]
    send_refs = refs[12:-3]
    cols, rows = e_ref.shape
    pair = 2 * share
    me = lax.axis_index("cols")
    core = me % 2
    entry = lax.broadcasted_iota(jnp.int32, (SUB, LANES), 1)
    for g in range(cols // (2 * SUB)):
        outs = []
        for h in range(2):
            s = pl.ds(g * 2 * SUB + h * SUB, SUB)
            outs.append(split_parts([ref[s, :] for ref in c_refs], entry, LEFT))
        left_ref[pl.ds(g * 2 * SUB, 2 * SUB), :] = jnp.concatenate(outs, axis=0).astype(BF16)
    for l in range(rows // LANES):
        ls = pl.ds(l * LANES, LANES)
        r = [wide(ref[:, ls]) for ref in r_refs] + [jnp.ones((SUB, LANES), F32)]
        for g in range(LANES // (2 * SUB)):
            outs = []
            for h in range(2):
                at = lax.broadcasted_iota(jnp.int32, (SUB, LANES), 0) + (2 * g + h) * SUB
                outs.append(split_parts(r, at, RIGHT) if (2 * g + h) * SUB < 36 else jnp.zeros((SUB, LANES), F32))
            right_ref[pl.ds(g * 2 * SUB, 2 * SUB), ls] = jnp.concatenate(outs, axis=0).astype(BF16)
    for p in range(rows // pair):
        lo = pl.multiple_of(((me // 2) ^ p) * pair, pair)
        block = pl.ds(lo, pair)
        for g in range(cols // MIX):
            s = pl.ds(g * MIX, MIX)
            scale = jnp.dot(left_ref[s, :], right_ref[:, block], preferred_element_type=F32)
            half_ref[s, block] = (e_ref[s, block] * scale).astype(BF16)
        if p % 2:
            products(share, pieces, p - 1, 1 - core, half_ref, y_ref, prod_ref, send_refs)


def products(share, pieces, p, side, half_ref, y_ref, prod_ref, out_refs):
    me = lax.axis_index("cols")
    pair = 2 * share
    split = share % LANES == 0
    size = share if split else pair
    blocks = []
    for q in range(2):
        lo = ((me // 2) ^ (p + q)) * pair + (side * share if split else 0)
        blocks.append(half_ref[:, pl.ds(pl.multiple_of(lo, LANES), size)])
    slot = p // 2 % 2
    prod_ref[slot] = lax.dot_general(
        jnp.concatenate(blocks, axis=1), y_ref[...], (((0,), (0,)), ((), ())),
        preferred_element_type=F32,
    )
    for q in range(2):
        at = q * size + (0 if split else side * share)
        for ref, (n, bits) in zip(out_refs, pieces):
            ref[spot(p + q, bits)] = prod_ref[slot, pl.ds(pl.multiple_of(at, SUB), n), :]
            at = at + n


def keep_kernel(share, pieces, half_ref, y_ref, *refs):
    core = lax.axis_index("cols") % 2
    for p in range(0, half_ref.shape[1] // (2 * share), 2):
        products(share, pieces, p, core, half_ref, y_ref, refs[-1], refs[:-1])


LEFT = (0, 0, 1, 0, 1, 2)
RIGHT = (0, 1, 0, 2, 1, 0)
MIX = 256


def split_parts(values, entry, which):
    x = jnp.zeros_like(values[0])
    for t, v in enumerate(values):
        x = jnp.where((entry >= 6 * t) & (entry < 6 * t + 6), v, x)
    first = x.astype(BF16).astype(F32)
    rest = x - first
    second = rest.astype(BF16).astype(F32)
    part = sum(jnp.where(entry % 6 == q, w, 0) for q, w in enumerate(which))
    return jnp.where(part == 0, first, jnp.where(part == 1, second, rest - second))


def spot(p, bits):
    return sum(bool(2 * p & k) << i for i, k in enumerate(reversed(bits)))


def product_shapes(share, pieces, rows, width):
    out = [jax.ShapeDtypeStruct((rows // (2 * share), n, width), F32) for n, _ in pieces]
    size = share if share % LANES == 0 else 2 * share
    return out, pltpu.VMEM((2, 2 * size, width), F32)


def mix(share, pieces, e, y, columns, weights):
    cols, rows = e.shape
    out, scratch = product_shapes(share, pieces, rows, y.shape[1])
    half, *sends = pl.pallas_call(
        functools.partial(mix_kernel, share, pieces),
        out_shape=(VMEM((cols, rows), BF16), *out),
        in_specs=full(13),
        out_specs=tuple(full(1 + len(out))),
        scratch_shapes=[
            scratch,
            pltpu.VMEM((cols, LANES), BF16),
            pltpu.VMEM((LANES, rows), BF16),
        ],
        compiler_params=params(16),
        name="mix",
    )(e, y, *columns, *weights)
    return half, sends


def keep(share, pieces, half, y):
    out, scratch = product_shapes(share, pieces, half.shape[1], y.shape[1])
    return pl.pallas_call(
        functools.partial(keep_kernel, share, pieces),
        out_shape=tuple(out),
        in_specs=full(2),
        out_specs=tuple(full(len(out))),
        scratch_shapes=[scratch],
        compiler_params=params(16),
        name="keep",
    )(half, y)


def back_kernel(total_cols, half_ref, x_ref, y_ref, e_ref, b_ref, r_ref, n_ref, sq_ref, bv2_ref,
                bv3_ref, mid_ref, gb1_ref, vbr_ref, w_ref, alpha_ref, u3_ref, weight_ref, mine_ref, after_ref,
                pot_ref, arch_ref, new_ref, base_ref, tmp_ref, col_ref):
    del after_ref
    share = mine_ref.shape[0]
    pair = 2 * share
    me = lax.axis_index("cols")
    lo = pl.multiple_of((me // 2) * pair, pair)
    for l in range(pair // LANES):
        at = pl.multiple_of(lo + l * LANES, LANES)
        col_ref[pl.ds(l * LANES, LANES), :] = column(weight_ref[:, pl.ds(at, LANES)])
    col = col_ref[pl.ds(pl.multiple_of((me % 2) * share, share), share), :]
    for l in range(mine_ref.shape[1] // LANES):
        ls = pl.ds(l * LANES, LANES)
        base_ref[:, ls] = col * mine_ref[:, ls]
    cols, rows = e_ref.shape
    width = y_ref.shape[1]
    column_dots(e_ref, [wide(a) for a in lanes(w_ref[...])], tmp_ref)
    step = 256
    for j in range(cols // step):
        s = pl.ds(j * step, step)
        b = b_ref[s, :]
        gb0 = vbr_ref[s, :] * spread(tmp_ref[s, :], jnp.sum)
        gb2 = mid_ref[s, :] * b / bv2_ref[s, :]
        tr = b + 2.0 * (gb2 + gb1_ref[s, :] / r_ref[s, :]) + gb0
        back = jnp.dot(half_ref[s, :], x_ref[...], preferred_element_type=F32)
        for l in range(width // LANES):
            ls = slice(l * LANES, (l + 1) * LANES)
            arch_ref[s, ls] = total_cols * (tr * y_ref[s, ls].astype(F32) - back[:, ls])
    for c in range(cols // LANES):
        s = pl.ds(c * LANES, LANES)
        pot = (sq_ref[s, :] - n_ref[s, :] + jnp.log2(bv3_ref[s, :] / b_ref[s, :])) * (1.0 / LOGK)
        pot_ref[:, s] = jnp.transpose(pot)[0:1, :]
    ones = jnp.ones((SUB, width), BF16)
    for i in range(rows // step):
        s = pl.ds(i * step, step)
        xf = x_ref[s, :].astype(F32)
        square = xf * xf
        high = square.astype(BF16)
        low = (square - high.astype(F32)).astype(BF16)
        sq = sum(
            lax.dot_general(ones, v, (((1,), (1,)), ((), ())), preferred_element_type=F32)
            for v in (high, low)
        )[0:1, :] * (LOGK / width)
        new_ref[:, s] = (alpha_ref[:, s] + jnp.log2(u3_ref[:, s]) + sq) * (1.0 / LOGK)


def back(total_cols, half, x, y, *rest, mine, after):
    cols, rows = half.shape
    width = y.shape[1]
    return pl.pallas_call(
        functools.partial(back_kernel, float(total_cols)),
        out_shape=(
            jax.ShapeDtypeStruct((1, cols), F32),
            jax.ShapeDtypeStruct((cols, width), F32),
            jax.ShapeDtypeStruct((1, rows), F32),
            VMEM(mine.shape, F32),
        ),
        in_specs=full(4 + len(rest)) + [pl.BlockSpec(memory_space=pl.ANY)],
        out_specs=tuple(full(4)),
        scratch_shapes=[
            pltpu.VMEM((cols, LANES), F32), pltpu.VMEM((2 * mine.shape[0], LANES), F32)
        ],
        compiler_params=params(16),
        cost_estimate=pl.CostEstimate(
            flops=2 * cols * rows * width, bytes_accessed=16 * 1024 * 1024, transcendentals=0
        ),
        name="back",
    )(half, x, y, *rest, mine, after)


def swap(v, k, count):
    return lax.ppermute(v, "cols", [(i, i ^ k) for i in range(count)])


def fold_kernel(keep_ref, got_ref, after_ref, stay_ref, away_ref):
    del after_ref
    half = keep_ref.shape[0] // 2
    for i in range(half):
        stay_ref[i] = keep_ref[i] + got_ref[i]
        away_ref[i] = keep_ref[half + i] + got_ref[half + i]


def fold(keep, got, after):
    blocks, n, width = keep.shape
    return pl.pallas_call(
        fold_kernel,
        out_shape=(jax.ShapeDtypeStruct((blocks // 2, n, width), F32),) * 2,
        in_specs=full(2) + [pl.BlockSpec(memory_space=pl.ANY)],
        out_specs=tuple(full(2)),
        compiler_params=params(8),
        name="fold",
    )(keep, got, after)


def scatter_sum(keeps, sends, pieces, count, after, meanwhile):
    keeps = list(keeps)
    gots = [swap(send, 1, count) for send in sends]

    def advance(i, step, after):
        keeps[i], away = fold(keeps[i], gots[i], after)
        gots[i] = swap(away, pieces[i][1][step], count)
        return away

    steps = count.bit_length() - 2
    other = None
    for t in range(steps + 1):
        turn = [(0, t), (1, t), (2, t)] if t == 0 else [(2, t), (0, t)] + [(1, t - 1)] * (t > 1)
        for i, step in turn:
            if step < steps:
                after = advance(i, step, after)
        if t == 0:
            other = meanwhile(after)
            after = other[-1]
    return [x[0] for pair in zip(keeps, gots) for x in pair], other


def gradient_kernel(pieces, scale, base_ref, *refs):
    terms, out_ref = refs[:-1], refs[-1]
    at = 0
    for i, (n, _) in enumerate(pieces):
        s = pl.ds(at, n)
        out_ref[s, :] = scale * (base_ref[s, :] - (terms[2 * i][...] + terms[2 * i + 1][...]))
        at += n


def gradient(pieces, scale, base, terms):
    return pl.pallas_call(
        functools.partial(gradient_kernel, pieces, float(scale)),
        out_shape=jax.ShapeDtypeStruct(base.shape, F32),
        in_specs=full(1 + len(terms)),
        out_specs=full(1)[0],
        compiler_params=params(8),
        name="gradient",
    )(base, *terms)


def combine(x, count, join):
    k = 1
    while k < count:
        if 4 * k <= count:
            x = join([x] + [swap(x, j * k, count) for j in (1, 2, 3)])
            k *= 4
        else:
            x = join([x, swap(x, k, count)])
            k *= 2
    return x


def add_join(xs):
    return tree(jnp.add, xs)


def lse_kernel(*refs):
    for l in range(refs[0].shape[1] // LANES):
        ls = pl.ds(l * LANES, LANES)
        xs = [ref[:, ls] for ref in refs[:-1]]
        m = tree(jnp.maximum, xs)
        refs[-1][:, ls] = m + jnp.log2(tree(jnp.add, [jnp.exp2(x - m) for x in xs]))


def lse_join(xs):
    return pl.pallas_call(
        lse_kernel,
        out_shape=jax.ShapeDtypeStruct(xs[0].shape, F32),
        in_specs=full(len(xs)),
        out_specs=full(1)[0],
        compiler_params=params(8),
        name="lse_join",
    )(*xs)


def routes(share, count):
    bits = [1 << i for i in range(1, count.bit_length() - 1)]
    units = share // SUB
    first = units * 6 // 16
    last = units - 2 * first
    return [(first * SUB, bits), (first * SUB, bits), (last * SUB, bits[1:] + bits[:1])]


def local(new_points, arch_points, new_mass, arch_mass):
    rows = new_points.shape[0]
    count = lax.axis_size("cols")
    assert count & (count - 1) == 0
    reduce_add = functools.partial(combine, count=count, join=add_join)
    reduce_lse = functools.partial(combine, count=count, join=lse_join)
    total_cols = arch_points.shape[0] * count
    share = rows // count
    a = (new_mass / rows).reshape(1, rows)

    z, b, sq, lse, mine = scores(new_points, arch_points, arch_mass, total_cols, share)
    alpha = -reduce_lse(lse)
    e, n, r, br, vbr, part = plan(z, b, sq, jnp.log2(a) + alpha)
    u2 = a / reduce_add(part)
    bv2, part = sweep("fwd", e, b, u2)
    u3 = a / reduce_add(part)
    bv3, part = sweep("fwd", e, b, u3)
    fbar3 = a + u3 * reduce_add(part)
    w3 = u3 * fbar3 / a
    mid, part = sweep("mid", e, b, bv2, w3)
    fbar2 = u2 * reduce_add(part)
    w2 = u2 * fbar2 / a
    gb1, part = sweep("bwd", e, br, r, w2)
    fbar1 = reduce_add(part)
    w1 = fbar1 / a
    pieces = routes(share, count)
    half, sends = mix(
        share, pieces, e, arch_points, (bv3, bv2, mid, br, vbr, gb1), (u3, w3, u2, w2, w1)
    )
    keeps = keep(share, pieces, half, arch_points)
    row_weight = 2.0 * (fbar3 + fbar2 + fbar1) - a
    terms, (pot, arch_grad, new_pot, base) = scatter_sum(
        keeps, sends, pieces, count, part,
        lambda after: back(
            total_cols, half, new_points, arch_points, e, b, r, n, sq, bv2, bv3, mid, gb1, vbr, w1,
            alpha, u3, row_weight, mine=mine, after=after
        ),
    )
    new_grad = gradient(pieces, rows, base, terms)
    return (new_pot.reshape(-1), pot.reshape(-1), new_grad, arch_grad)


def solution(mesh):
    in_specs = (P("pairs", None), P(("pairs", "cols"), None), P("pairs"), P(("pairs", "cols")))
    out_specs = (
        P("pairs"),
        P(("pairs", "cols")),
        P(("pairs", "cols"), None),
        P(("pairs", "cols"), None),
    )
    return jax.shard_map(local, mesh=mesh, in_specs=in_specs, out_specs=out_specs, check_vma=False)
```
